256 devices in a mesh: dp: 16 (over y_hi, x, core), mp: 16 (over y_lo, z).
Axes of the slice: x: 4, y: 4 (y_hi: 2, y_lo: 2; y = y_hi * 2 + y_lo), z: 8, core: 2. Of those that a mesh axis runs over, the one named last changes fastest.
Arguments:
- series: bfloat16 [16, 2048, 16, 256], P('dp', 'mp'), may hold values from -6 to 6
- upstream_grad: bfloat16 [16, 2048, 16, 256], P('dp', None, 'mp'), may hold values from -3 to 3
- time_weights: bfloat16 [4, 256, 256], replicated, may hold values from -0.375 to 0.375
- channel_weights: bfloat16 [4, 256, 256], replicated, may hold values from -0.375 to 0.375
- neighbors: int32 [16, 3], replicated, may hold values from 0 to 15, as said below
Outputs:
- mixed_series: bfloat16 [16, 2048, 16, 256], P('dp', None, 'mp')
- series_grad: bfloat16 [16, 2048, 16, 256], P('dp', 'mp')
- time_grads: float32 [4, 256, 256], P(None, 'mp')
- channel_grads: float32 [4, 256, 256], P(None, 'mp')
The draws below stay inside these ranges and needn't reach their ends.
Inputs may be any that keep to these rules, and one draw needn't show every extreme that they name: `neighbors`: row b names 3 different blocks; its first entry is b.
All inputs are finite; a program needn't handle non-finite values.
Results may differ from the reference program's by a relative error of at most 0.025.
Values may be sent and summed in bfloat16 or wider, within the bound.
No kernel may reach another device: no remote copies, remote signals or barrier semaphores. Data moves between devices by JAX's collectives and lax.ppermute only.
A program may use at most 192 MiB of HBM per device.

```python
import jax
import jax.numpy as jnp
from jax import lax

D = 256
HEADS = 4
NBR = 3
L = 16
B = 16
C = 2048
BLOCKS = 16


def draw_neighbors(key, part):
    attention_logits = jax.random.randint(key, (BLOCKS, BLOCKS), 0, 4096, dtype=jnp.int32)
    columns = jnp.arange(BLOCKS, dtype=jnp.int32)
    attention_logits = attention_logits * BLOCKS + columns[None, :]
    attention_logits = jnp.where(columns[None, :] == columns[:, None], jnp.int32(1 << 30), attention_logits)
    order = jnp.argsort(attention_logits, axis=1, stable=True).astype(jnp.int32)
    return jnp.concatenate([columns[:, None], order[:, :NBR - 1]], axis=1).astype(jnp.int32)


def level_of(key, shape, split, smallest, largest):
    gain = 1.0
    for axis_at, blocks in split:
        steps = jax.random.uniform(jax.random.fold_in(jax.random.fold_in(key, 6), axis_at), (blocks,), jnp.float32, smallest / len(split), largest / len(split))
        gain = gain * jnp.repeat(jnp.exp(steps), shape[axis_at] // blocks).reshape((-1,) + (1,) * (len(shape) - 1 - axis_at))
    return gain


def normal_values(rng, extent, spread, limit, cuts=(), held_as=jnp.bfloat16):
    entries = spread * jax.random.normal(rng, extent, jnp.float32)
    if cuts:
        entries = entries * level_of(rng, extent, cuts, -0.22, 0.18)
    return jnp.clip(entries, -limit, limit).astype(held_as)


def setup_inputs(seed: int = 0) -> dict:
    key_list = jax.random.split(jax.random.key(seed), 6)
    return {
        "series": normal_values(key_list[0], (B, C, L, D), 1.0, 6.0, ((0, 16), (1, 16))),
        "upstream_grad": normal_values(key_list[1], (B, C, L, D), 0.5, 3.0, ((0, 16), (2, 16))),
        "time_weights": normal_values(key_list[2], (4, D, D), D ** -0.5, 0.375),
        "channel_weights": normal_values(key_list[3], (4, D, D), D ** -0.5, 0.375),
        "neighbors": draw_neighbors(jax.random.fold_in(key_list[5], 71), 0),
    }


EPS = 1e-06
LOGIT_SCALE = 0.25

def cast_to_single_float(values):
    return values.astype(jnp.float32)

def cast_to_brain_float(values):
    return lax.optimization_barrier(values.astype(jnp.bfloat16))

def row_norm(inputs):
    return inputs * lax.rsqrt(lax.optimization_barrier(jnp.mean(inputs * inputs, axis=-1, keepdims=True)) + EPS)

def head_norm(inputs):
    shaped = inputs.reshape(inputs.shape[:-1] + (HEADS, inputs.shape[-1] // HEADS))
    return row_norm(shaped).reshape(inputs.shape)

def project(normed, weights):
    raw_query = jnp.dot(normed, weights[0], preferred_element_type=jnp.float32)
    raw_key = jnp.dot(normed, weights[1], preferred_element_type=jnp.float32)
    value_rows = cast_to_brain_float(jnp.dot(normed, weights[2], preferred_element_type=jnp.float32))
    query_rows = cast_to_brain_float(head_norm(raw_query))
    key_rows = cast_to_brain_float(head_norm(raw_key))
    return (raw_query, raw_key, query_rows, key_rows, value_rows)

def project_back(normed, raw_query, raw_key, query_grad, key_grad, value_grad, weights):
    query_back = cast_to_brain_float(jax.vjp(head_norm, raw_query)[1](query_grad)[0])
    key_back = cast_to_brain_float(jax.vjp(head_norm, raw_key)[1](key_grad)[0])
    value_back = cast_to_brain_float(value_grad)
    weight_grads = [jnp.dot(normed.T, back_rows, preferred_element_type=jnp.float32) for back_rows in (query_back, key_back, value_back)]
    normed_grad = jnp.dot(query_back, weights[0].T, preferred_element_type=jnp.float32)
    normed_grad = normed_grad + jnp.dot(key_back, weights[1].T, preferred_element_type=jnp.float32)
    normed_grad = normed_grad + jnp.dot(value_back, weights[2].T, preferred_element_type=jnp.float32)
    return (normed_grad, weight_grads)

def attend_time(query_heads, key_heads, value_heads):
    attention_logits = LOGIT_SCALE * jnp.einsum('clhe,cmhe->hlmc', cast_to_single_float(query_heads), cast_to_single_float(key_heads))
    exponent = jnp.exp(attention_logits)
    attention_layer = exponent / lax.optimization_barrier(jnp.sum(exponent, axis=2, keepdims=True))
    weights_brain_float = cast_to_brain_float(attention_layer)
    mixed_heads = jnp.einsum('hlmc,cmhe->clhe', cast_to_single_float(weights_brain_float), cast_to_single_float(value_heads))
    return (cast_to_brain_float(mixed_heads), attention_layer)

def revert_time(query_heads, key_heads, value_heads, attention_layer, grad_heads):
    weights_brain_float = cast_to_brain_float(attention_layer)
    attention_gradient = jnp.einsum('clhe,cmhe->hlmc', cast_to_single_float(grad_heads), cast_to_single_float(value_heads))
    row_delta = lax.optimization_barrier(jnp.sum(attention_layer * attention_gradient, axis=2, keepdims=True))
    logit_gradient = cast_to_brain_float(LOGIT_SCALE * attention_layer * (attention_gradient - row_delta))
    query_grad = jnp.einsum('hlmc,cmhe->clhe', cast_to_single_float(logit_gradient), cast_to_single_float(key_heads))
    key_grad = jnp.einsum('hlmc,clhe->cmhe', cast_to_single_float(logit_gradient), cast_to_single_float(query_heads))
    value_grad = jnp.einsum('hlmc,clhe->cmhe', cast_to_single_float(weights_brain_float), cast_to_single_float(grad_heads))
    return (query_grad, key_grad, value_grad)

def forward_time(series_rows, weights):
    channel_count, length, features = series_rows.shape
    total_rows = channel_count * length
    normed = cast_to_brain_float(row_norm(cast_to_single_float(series_rows))).reshape(total_rows, features)
    raw_query, raw_key, query_rows, key_rows, value_rows = project(normed, weights)
    shaped = (channel_count, length, HEADS, features // HEADS)
    mixed_heads, attention_layer = attend_time(query_rows.reshape(shaped), key_rows.reshape(shaped), value_rows.reshape(shaped))
    mixed_flat = mixed_heads.reshape(total_rows, features)
    branch = jnp.dot(mixed_flat, weights[3], preferred_element_type=jnp.float32).reshape(series_rows.shape)
    stream = cast_to_brain_float(cast_to_single_float(series_rows) + branch)
    return (stream, (normed, raw_query, raw_key, query_rows, key_rows, value_rows, mixed_flat, attention_layer))

def backward_time(series_rows, stored, stream_grad, weights):
    normed, raw_query, raw_key, query_rows, key_rows, value_rows, mixed_flat, attention_layer = stored
    channel_count, length, features = series_rows.shape
    total_rows = channel_count * length
    shaped = (channel_count, length, HEADS, features // HEADS)
    grad_flat = stream_grad.reshape(total_rows, features)
    out_grad = jnp.dot(mixed_flat.T, grad_flat, preferred_element_type=jnp.float32)
    mixed_grad = cast_to_brain_float(jnp.dot(grad_flat, weights[3].T, preferred_element_type=jnp.float32))
    query_grad, key_grad, value_grad = revert_time(query_rows.reshape(shaped), key_rows.reshape(shaped), value_rows.reshape(shaped), attention_layer, mixed_grad.reshape(shaped))
    normed_grad, weight_grads = project_back(normed, raw_query, raw_key, query_grad.reshape(total_rows, features), key_grad.reshape(total_rows, features), value_grad.reshape(total_rows, features), weights)
    norm_back = jax.vjp(row_norm, cast_to_single_float(series_rows))[1]
    series_grad = cast_to_brain_float(cast_to_single_float(stream_grad) + norm_back(normed_grad.reshape(series_rows.shape))[0])
    return (series_grad, jnp.stack(weight_grads + [out_grad]))

def near_blocks(source_rows, neighbors):
    block_list = neighbors.shape[0]
    shaped = source_rows.reshape(block_list, source_rows.shape[0] // block_list, source_rows.shape[1])
    return shaped[neighbors].reshape(block_list, -1, source_rows.shape[1])

def attend_channels(query_rows, key_rows, value_rows, neighbors):
    block_list = neighbors.shape[0]
    features = query_rows.shape[1]
    head_width = features // HEADS
    query_blocks = query_rows.reshape(block_list, -1, features)
    key_near = near_blocks(key_rows, neighbors)
    value_near = near_blocks(value_rows, neighbors)
    per_head_output = []
    for head_number in range(HEADS):
        first_col = head_number * head_width
        single_query_head = query_blocks[:, :, first_col:first_col + head_width]
        single_key_head = key_near[:, :, first_col:first_col + head_width]
        single_value_head = value_near[:, :, first_col:first_col + head_width]
        attention_logits = LOGIT_SCALE * jnp.einsum('fdr,fwr->fdw', cast_to_single_float(single_query_head), cast_to_single_float(single_key_head))
        exponent = jnp.exp(attention_logits)
        attention_layer = exponent / lax.optimization_barrier(jnp.sum(exponent, axis=2, keepdims=True))
        per_head_output.append(jnp.einsum('xlj,xjr->xlr', cast_to_single_float(cast_to_brain_float(attention_layer)), cast_to_single_float(single_value_head)))
    return cast_to_brain_float(jnp.concatenate(per_head_output, axis=2).reshape(query_rows.shape))

def join_heads(head_parts, shape):
    return jnp.concatenate(head_parts, axis=2).reshape(shape)

def revert_channels(query_rows, key_rows, value_rows, neighbors, mixed_grad):
    block_list, neighbor_count = neighbors.shape
    features = query_rows.shape[1]
    head_width = features // HEADS
    block_length = query_rows.shape[0] // block_list
    onehot = (neighbors.reshape(-1)[:, None] == jnp.arange(block_list, dtype=jnp.int32)[None, :]).astype(jnp.float32)
    query_blocks = query_rows.reshape(block_list, -1, features)
    grad_blocks = mixed_grad.reshape(block_list, -1, features)
    key_near = near_blocks(key_rows, neighbors)
    value_near = near_blocks(value_rows, neighbors)
    query_pieces_list, key_parts, value_parts = ([], [], [])
    for head_number in range(HEADS):
        first_col = head_number * head_width
        single_query_head = query_blocks[:, :, first_col:first_col + head_width]
        single_key_head = key_near[:, :, first_col:first_col + head_width]
        single_value_head = value_near[:, :, first_col:first_col + head_width]
        head_gradient = grad_blocks[:, :, first_col:first_col + head_width]
        attention_logits = LOGIT_SCALE * jnp.einsum('fdr,fwr->fdw', cast_to_single_float(single_query_head), cast_to_single_float(single_key_head))
        exponent = jnp.exp(attention_logits)
        attention_layer = exponent / lax.optimization_barrier(jnp.sum(exponent, axis=2, keepdims=True))
        weights_brain_float = cast_to_brain_float(attention_layer)
        attention_gradient = jnp.einsum('fdr,fwr->fdw', cast_to_single_float(head_gradient), cast_to_single_float(single_value_head))
        row_delta = lax.optimization_barrier(jnp.sum(attention_layer * attention_gradient, axis=2, keepdims=True))
        logit_gradient = cast_to_brain_float(LOGIT_SCALE * attention_layer * (attention_gradient - row_delta))
        query_pieces_list.append(jnp.einsum('xlj,xjr->xlr', cast_to_single_float(logit_gradient), cast_to_single_float(single_key_head)))
        neighbor_key_gradient = jnp.einsum('tsa,tsg->tag', cast_to_single_float(logit_gradient), cast_to_single_float(single_query_head)).reshape(block_list * neighbor_count, block_length, head_width)
        neighbor_value_gradient = jnp.einsum('tsa,tsg->tag', cast_to_single_float(weights_brain_float), cast_to_single_float(head_gradient)).reshape(block_list * neighbor_count, block_length, head_width)
        key_parts.append(jnp.einsum('ob,ote->bte', onehot, neighbor_key_gradient, precision=lax.Precision.HIGHEST))
        value_parts.append(jnp.einsum('ob,ote->bte', onehot, neighbor_value_gradient, precision=lax.Precision.HIGHEST))
    shape = query_rows.shape
    return (join_heads(query_pieces_list, shape), join_heads(key_parts, shape), join_heads(value_parts, shape))

def forward_channels(stream_rows, weights, neighbors):
    stream_float = cast_to_single_float(stream_rows)
    normed = cast_to_brain_float(row_norm(stream_float))
    raw_query, raw_key, query_rows, key_rows, value_rows = project(normed, weights)
    mixed_rows = attend_channels(query_rows, key_rows, value_rows, neighbors)
    output_rows = cast_to_brain_float(stream_float + jnp.dot(mixed_rows, weights[3], preferred_element_type=jnp.float32))
    return (output_rows, normed, raw_query, raw_key, value_rows, mixed_rows)

def backward_channels(stream_rows, normed, raw_query, raw_key, value_rows, mixed_rows, upstream_rows, weights, neighbors):
    out_grad = jnp.dot(mixed_rows.T, upstream_rows, preferred_element_type=jnp.float32)
    mixed_grad = cast_to_brain_float(jnp.dot(upstream_rows, weights[3].T, preferred_element_type=jnp.float32))
    query_rows = cast_to_brain_float(head_norm(raw_query))
    key_rows = cast_to_brain_float(head_norm(raw_key))
    query_grad, key_grad, value_grad = revert_channels(query_rows, key_rows, value_rows, neighbors, mixed_grad)
    normed_grad, weight_grads = project_back(normed, raw_query, raw_key, query_grad, key_grad, value_grad, weights)
    norm_back = jax.vjp(row_norm, cast_to_single_float(stream_rows))[1]
    stream_grad = cast_to_brain_float(cast_to_single_float(upstream_rows) + norm_back(normed_grad)[0])
    return (stream_grad, jnp.stack(weight_grads + [out_grad]))

def reference(series, upstream_grad, time_weights, channel_weights, neighbors):

    def sample_pass(sample_pair):
        series_rows, upstream_rows = sample_pair
        stream, stored = forward_time(series_rows, time_weights)

        def segment_pass(segment_pair):
            stream_seg, upstream_seg = segment_pair
            output_rows, normed, raw_query, raw_key, value_rows, mixed_rows = forward_channels(stream_seg, channel_weights, neighbors)
            stream_grad, grad_stack = backward_channels(stream_seg, normed, raw_query, raw_key, value_rows, mixed_rows, upstream_seg, channel_weights, neighbors)
            return (output_rows, stream_grad, grad_stack)
        outputs, stream_grads, channel_parts = lax.map(segment_pass, (jnp.swapaxes(stream, 0, 1), jnp.swapaxes(upstream_rows, 0, 1)))
        series_grad, time_part = backward_time(series_rows, stored, jnp.swapaxes(stream_grads, 0, 1), time_weights)
        return (jnp.swapaxes(outputs, 0, 1), series_grad, time_part, lax.optimization_barrier(jnp.sum(channel_parts, axis=0)))
    mixed_series, series_grad, time_parts, channel_parts = lax.map(sample_pass, (series, upstream_grad))
    time_grads = lax.optimization_barrier(jnp.sum(time_parts, axis=0)) / B
    channel_grads = lax.optimization_barrier(jnp.sum(channel_parts, axis=0)) / B
    return (mixed_series, series_grad, time_grads, channel_grads)
```

```python
import jax
import jax.numpy as jnp
from jax import lax
from jax.experimental import pallas as pl
from jax.experimental.pallas import tpu as pltpu
from jax.sharding import PartitionSpec as P

HEADS = 4
D = 256
HD = D // HEADS
L = 16
CH = 128
BLK = 128
NBR = 3
ROWS = 2048
STEP = 256
STEPS = ROWS // STEP
EPS = 1e-06
LOG2E = 1.4426950408889634
LN2 = 0.6931471805599453
QSCALE = 0.25 * LOG2E
F32 = jnp.float32
BF16 = jnp.bfloat16


def dot(a, b):
    return lax.dot_general(a, b, (((1,), (0,)), ((), ())), preferred_element_type=F32)


def dot_rt(a, b):
    return lax.dot_general(a, b, (((1,), (1,)), ((), ())), preferred_element_type=F32)


def dot_lt(a, b):
    return lax.dot_general(a, b, (((0,), (0,)), ((), ())), preferred_element_type=F32)


def iota(shape, dim):
    return lax.broadcasted_iota(jnp.int32, shape, dim)


def div(a, n):
    return lax.shift_right_logical(a, jnp.int32(n.bit_length() - 1))


def head_mean_matrix():
    same = div(iota((D, D), 0), HD) == div(iota((D, D), 1), HD)
    return jnp.where(same, 1.0 / HD, 0.0).astype(BF16)


def swap_matrix():
    row, col = iota((D, D), 0), iota((D, D), 1)
    same = (div(row, L) == (col & (L - 1))) & ((row & (L - 1)) == div(col, L))
    return jnp.where(same, 1.0, 0.0).astype(BF16)


def rms_scale(x):
    return lax.rsqrt(jnp.mean(x * x, axis=-1, keepdims=True) + EPS)


def head_scale(raw, means):
    return lax.rsqrt(dot((raw * raw).astype(BF16), means) + EPS)


def project(xn, wqkv, means):
    qkv = dot(xn, wqkv)
    raw_q, raw_k = qkv[:, :D], qkv[:, D : 2 * D]
    rq, rk = head_scale(raw_q, means), head_scale(raw_k, means)
    qs = (raw_q * (rq * QSCALE)).astype(BF16)
    kn = (raw_k * rk).astype(BF16)
    return qs, kn, qkv[:, 2 * D :].astype(BF16), rq, rk


def head_masks(rows):
    lane = div(iota((rows, D), 1), HD)
    return [lane == h for h in range(HEADS)]


def stack_heads(x, masks):
    zero = jnp.zeros_like(x)
    return jnp.concatenate([jnp.where(m, x, zero) for m in masks], axis=0)


def time_consts():
    row, col = iota((BLK, HEADS * BLK), 0), iota((BLK, HEADS * BLK), 1)
    diag = jnp.where(div(row, L) == div(col & (BLK - 1), L), 1.0, 0.0).astype(F32)
    ones = jnp.where(
        div(iota((HEADS * BLK, D), 0), BLK) == div(iota((HEADS * BLK, D), 1), HD), 1.0, 0.0
    ).astype(BF16)
    return diag, ones


def time_attend(q, k, v, masks, diag, ones):
    kst, vst = stack_heads(k, masks), stack_heads(v, masks)
    e = jnp.exp2(dot_rt(q, kst)) * diag
    eb = e.astype(BF16)
    rden = 1.0 / dot(eb, ones)
    return e, eb, dot(eb, vst) * rden, rden, kst, vst


def load_wqkv(w_ref):
    return jnp.concatenate([w_ref[0], w_ref[1], w_ref[2]], axis=1)


def time_forward_kernel(x_ref, w_ref, out_ref):
    means, swap = head_mean_matrix(), swap_matrix()
    masks = head_masks(BLK)
    diag, ones = time_consts()
    wqkv = load_wqkv(w_ref)
    wo = w_ref[3]

    def step(i, _):
        x = x_ref[pl.ds(i * STEP, STEP), :].astype(F32)
        xn = (x * rms_scale(x)).astype(BF16)
        qs, kn, v, _, _ = project(xn, wqkv, means)
        mixed = []
        for g in range(STEP // BLK):
            rows = slice(g * BLK, (g + 1) * BLK)
            o = time_attend(qs[rows], kn[rows], v[rows], masks, diag, ones)[2]
            mixed.append(o.astype(BF16))
        stream = (x + dot(jnp.concatenate(mixed, axis=0), wo)).astype(BF16)
        out = dot(swap, stream).astype(BF16)
        out_ref[:, pl.ds(i * L, L), :] = out.reshape(L, STEP // L, D)
        return 0

    lax.fori_loop(0, STEPS, step, 0)


def head_norm_back(r, y, g, means):
    return r * (g - y * dot((y * g).astype(BF16), means))


def query_back(rq, qs, dq, means):
    qf = qs.astype(F32)
    m = dot((qf * dq).astype(BF16), means)
    return (rq * 0.25) * (dq - qf * (m * (1.0 / (QSCALE * QSCALE))))


def key_back(rk, kn, dk, means):
    kf = kn.astype(F32)
    m = dot((kf * dk).astype(BF16), means)
    return (rk * LN2) * (dk - kf * m)


def rms_back(x, r, ng):
    xh = x * r
    return r * (ng - xh * jnp.mean(xh * ng, axis=-1, keepdims=True))


def time_backward_kernel(x_ref, sg_ref, w_ref, out_ref, grads_ref, acc, acc_o):
    means, swap = head_mean_matrix(), swap_matrix()
    masks = head_masks(BLK)
    diag, ones = time_consts()
    spread = jnp.where(
        div(iota((D, HEADS * BLK), 0), HD) == div(iota((D, HEADS * BLK), 1), BLK), 1.0, 0.0
    ).astype(BF16)
    wqkv = load_wqkv(w_ref)
    wo = w_ref[3]
    acc[...] = jnp.zeros_like(acc)
    acc_o[...] = jnp.zeros_like(acc_o)

    def step(i, _):
        x = x_ref[pl.ds(i * STEP, STEP), :].astype(F32)
        r = rms_scale(x)
        xn = (x * r).astype(BF16)
        qs, kn, v, rq, rk = project(xn, wqkv, means)
        sg = sg_ref[:, pl.ds(i * L, L), :].reshape(STEP, D)
        sgf = dot(swap, sg)
        sg = sgf.astype(BF16)
        do = dot_rt(sg, wo)
        mixed, dqs, dks, dvs = [], [], [], []
        for g in range(STEP // BLK):
            rows = slice(g * BLK, (g + 1) * BLK)
            q = qs[rows]
            e, eb, o, rden, kst, vst = time_attend(q, kn[rows], v[rows], masks, diag, ones)
            mixed.append(o.astype(BF16))
            dof = do[rows] * rden
            dob = dof.astype(BF16)
            dp = dot_rt(dob, vst) - dot((dof * o).astype(BF16), spread)
            ds = (e * dp).astype(BF16)
            dqs.append(dot(ds, kst))
            cols = [slice(h * BLK, (h + 1) * BLK) for h in range(HEADS)]
            dsr = jnp.concatenate([ds[:, c] for c in cols], axis=0)
            ebr = jnp.concatenate([eb[:, c] for c in cols], axis=0)
            dks.append(dot_lt(dsr, stack_heads(q, masks)))
            dvs.append(dot_lt(ebr, stack_heads(dob, masks)))
        mixed = jnp.concatenate(mixed, axis=0)
        qb = query_back(rq, qs, jnp.concatenate(dqs, axis=0), means).astype(BF16)
        kb = key_back(rk, kn, jnp.concatenate(dks, axis=0), means).astype(BF16)
        vb = jnp.concatenate(dvs, axis=0).astype(BF16)
        back = jnp.concatenate([qb, kb, vb], axis=1)
        ng = dot_rt(back, wqkv)
        out_ref[pl.ds(i * STEP, STEP), :] = (sgf + rms_back(x, r, ng)).astype(BF16)
        acc[...] += dot_lt(xn, back)
        acc_o[...] += dot_lt(mixed, sg)
        return 0

    lax.fori_loop(0, STEPS, step, 0)
    for j in range(3):
        grads_ref[:, j] = acc[:, j * D : (j + 1) * D].astype(BF16).reshape(16, 16, D)
    grads_ref[:, 3] = acc_o[...].astype(BF16).reshape(16, 16, D)


def channel_kernel(
    nb_ref, x_ref, up_ref, w_ref, sg_ref, back_ref, mixed_ref,
    qs_s, kn_s, v_s, do_s, rq_s, rk_s, dq_s, dk_s, dv_s,
):
    means = head_mean_matrix()
    masks = head_masks(BLK)
    wqkv = load_wqkv(w_ref)
    wo = w_ref[3]

    def first(i, _):
        at = pl.ds(i * STEP, STEP)
        x = x_ref[at, :].astype(F32)
        xn = (x * rms_scale(x)).astype(BF16)
        qs_s[at, :], kn_s[at, :], v_s[at, :], rq_s[at, :], rk_s[at, :] = project(xn, wqkv, means)
        do_s[at, :] = dot_rt(up_ref[at, :], wo).astype(BF16)
        dk_s[at, :] = jnp.zeros((STEP, D), F32)
        dv_s[at, :] = jnp.zeros((STEP, D), F32)
        return 0

    lax.fori_loop(0, STEPS, first, 0)

    def pick(parts):
        out = parts[0]
        for h in range(1, HEADS):
            out = jnp.where(masks[h], parts[h], out)
        return out

    def heads_of(x):
        return [x[h * BLK : (h + 1) * BLK] for h in range(HEADS)]

    def attend(b, _):
        at = pl.ds(b * BLK, BLK)
        near = [pl.ds(pl.multiple_of(nb_ref[b, j] * BLK, BLK), BLK) for j in range(NBR)]
        k = jnp.concatenate([kn_s[n, :] for n in near], axis=0)
        v = jnp.concatenate([v_s[n, :] for n in near], axis=0)
        qst = stack_heads(qs_s[at, :], masks)
        e = jnp.exp2(dot_rt(qst, k))
        rden = 1.0 / jnp.sum(e, axis=-1, keepdims=True)
        eb = e.astype(BF16)
        rdens = heads_of(rden)
        scale = pick([jnp.broadcast_to(d, (BLK, D)) for d in rdens])
        o = pick(heads_of(dot(eb, v))) * scale
        mixed_ref[at, :] = o.astype(BF16)
        dof = do_s[at, :].astype(F32) * scale
        prod = dof * o
        zero = jnp.zeros_like(prod)
        delta = jnp.concatenate(
            [jnp.sum(jnp.where(m, prod, zero), axis=-1, keepdims=True) for m in masks], axis=0
        )
        dost = stack_heads(dof.astype(BF16), masks)
        ds = (e * (dot_rt(dost, v) - delta)).astype(BF16)
        dq_s[at, :] = pick(heads_of(dot(ds, k)))
        dk = dot_lt(ds, qst)
        dv = dot_lt(eb, dost)
        for j, n in enumerate(near):
            rows = slice(j * BLK, (j + 1) * BLK)
            dk_s[n, :] += dk[rows]
            dv_s[n, :] += dv[rows]
        return 0

    lax.fori_loop(0, ROWS // BLK, attend, 0)

    def last(i, _):
        at = pl.ds(i * STEP, STEP)
        x = x_ref[at, :].astype(F32)
        r = rms_scale(x)
        qb = query_back(rq_s[at, :], qs_s[at, :], dq_s[at, :], means).astype(BF16)
        kb = key_back(rk_s[at, :], kn_s[at, :], dk_s[at, :], means).astype(BF16)
        back = jnp.concatenate([qb, kb, dv_s[at, :].astype(BF16)], axis=1)
        back_ref[at, :] = back
        dx = rms_back(x, r, dot_rt(back, wqkv))
        sg_ref[at, :] = (up_ref[at, :].astype(F32) + dx).astype(BF16)
        return 0

    lax.fori_loop(0, STEPS, last, 0)


def channel_grads_kernel(x_ref, up_ref, back_ref, mixed_ref, w_ref, out_ref, grads_ref, acc, acc_o):
    wo = w_ref[3]
    acc[...] = jnp.zeros_like(acc)
    acc_o[...] = jnp.zeros_like(acc_o)

    def step(i, _):
        at = pl.ds(i * STEP, STEP)
        x = x_ref[at, :].astype(F32)
        xn = (x * rms_scale(x)).astype(BF16)
        mixed = mixed_ref[at, :]
        out_ref[at, :] = (x + dot(mixed, wo)).astype(BF16)
        acc[...] += dot_lt(xn, back_ref[at, :])
        acc_o[...] += dot_lt(mixed, up_ref[at, :])
        return 0

    lax.fori_loop(0, STEPS, step, 0)
    for j in range(3):
        grads_ref[:, j] = acc[:, j * D : (j + 1) * D].astype(BF16).reshape(16, 16, D)
    grads_ref[:, 3] = acc_o[...].astype(BF16).reshape(16, 16, D)


def vmem(n=None):
    return pl.BlockSpec(memory_space=pltpu.VMEM)


def shape(dims, dtype=BF16):
    return jax.ShapeDtypeStruct(dims, dtype)


def params(mib):
    return pltpu.CompilerParams(vmem_limit_bytes=mib << 20)


def time_forward(x, w):
    return pl.pallas_call(
        time_forward_kernel,
        out_shape=shape((L, CH, D)),
        in_specs=[vmem(), vmem()],
        out_specs=vmem(),
        compiler_params=params(24),
        name="time_forward",
    )(x, w)


def time_backward(x, sg, w):
    return pl.pallas_call(
        time_backward_kernel,
        out_shape=(shape((ROWS, D)), shape((16, 4, 16, D))),
        in_specs=[vmem()] * 3,
        out_specs=(vmem(), vmem()),
        scratch_shapes=[pltpu.VMEM((D, 3 * D), F32), pltpu.VMEM((D, D), F32)],
        compiler_params=params(24),
        name="time_backward",
    )(x, sg, w)


def channel(nb, x, up, w):
    return pl.pallas_call(
        channel_kernel,
        out_shape=(shape((ROWS, D)), shape((ROWS, 3 * D)), shape((ROWS, D))),
        in_specs=[pl.BlockSpec(memory_space=pltpu.SMEM)] + [vmem()] * 3,
        out_specs=(vmem(),) * 3,
        scratch_shapes=[pltpu.VMEM((ROWS, D), BF16)] * 4 + [pltpu.VMEM((ROWS, D), F32)] * 5,
        compiler_params=params(40),
        name="channel",
    )(nb, x, up, w)


def channel_grads(x, up, back, mixed, w):
    return pl.pallas_call(
        channel_grads_kernel,
        out_shape=(shape((ROWS, D)), shape((16, 4, 16, D))),
        in_specs=[vmem()] * 5,
        out_specs=(vmem(), vmem()),
        scratch_shapes=[pltpu.VMEM((D, 3 * D), F32), pltpu.VMEM((D, D), F32)],
        compiler_params=params(24),
        name="channel_grads",
    )(x, up, back, mixed, w)


def exchange(x, axis):
    return lax.all_to_all(x, axis, split_axis=0, concat_axis=0, tiled=True)


def reduce_grads(parts):
    rows = exchange(parts, "mp")
    mine = jnp.sum(rows.astype(F32), axis=0).astype(BF16)
    every = exchange(jnp.broadcast_to(mine[None], parts.shape), "dp")
    return jnp.sum(every.astype(F32), axis=0) * (1.0 / 16)


def shards(series, upstream_grad, time_weights, channel_weights, neighbors):
    x = series.reshape(ROWS, D)
    up = upstream_grad.reshape(ROWS, D)
    stream = exchange(time_forward(x, time_weights), "mp").reshape(ROWS, D)
    sg, back, mixed = channel(neighbors, stream, up, channel_weights)
    returned = exchange(sg.reshape(16, CH, D), "mp")
    out, cparts = channel_grads(stream, up, back, mixed, channel_weights)
    cgrads = reduce_grads(cparts)
    sgrad, tparts = time_backward(x, returned, time_weights)
    tgrads = reduce_grads(tparts)
    return (
        out.reshape(1, ROWS, 1, D),
        sgrad.reshape(1, CH, L, D),
        tgrads,
        cgrads,
    )


def solution(mesh):
    placed = (P("dp", "mp", None, None), P("dp", None, "mp", None), P(), P(), P())
    return jax.shard_map(
        shards,
        mesh=mesh,
        in_specs=placed,
        out_specs=(
            P("dp", None, "mp", None),
            P("dp", "mp", None, None),
            P(None, "mp", None),
            P(None, "mp", None),
        ),
        check_vma=False,
    )
```

```python
import jax
import jax.numpy as jnp
from jax import lax
from jax.experimental import pallas as pl
from jax.experimental.pallas import tpu as pltpu
from jax.sharding import PartitionSpec as P

HEADS = 4
D = 256
HD = D // HEADS
L = 16
CH = 128
BLK = 128
NBR = 3
ROWS = 2048
SQ = 256
GROUPS = 2
EPS = 1e-06
LOG2E = 1.4426950408889634
LN2 = 0.6931471805599453
QSCALE = 0.25 * LOG2E
F32 = jnp.float32
BF16 = jnp.bfloat16


def dot(a, b):
    return lax.dot_general(a, b, (((1,), (0,)), ((), ())), preferred_element_type=F32)


def dot_rt(a, b):
    return lax.dot_general(a, b, (((1,), (1,)), ((), ())), preferred_element_type=F32)


def dot_lt(a, b):
    return lax.dot_general(a, b, (((0,), (0,)), ((), ())), preferred_element_type=F32)


def iota(shape, dim):
    return lax.broadcasted_iota(jnp.int32, shape, dim)


def div(a, n):
    return lax.shift_right_logical(a, jnp.int32(n.bit_length() - 1))


def head_mean_matrix():
    same = div(iota((D, D), 0), HD) == div(iota((D, D), 1), HD)
    return jnp.where(same, 1.0 / HD, 0.0).astype(BF16)


def swap_matrix():
    row, col = iota((D, D), 0), iota((D, D), 1)
    same = (div(row, L) == (col & (L - 1))) & ((row & (L - 1)) == div(col, L))
    return jnp.where(same, 1.0, 0.0).astype(BF16)


def rms_scale(x):
    return lax.rsqrt(jnp.mean(x * x, axis=-1, keepdims=True) + EPS)


def head_scale(raw, means):
    return lax.rsqrt(dot((raw * raw).astype(BF16), means) + EPS)


def project(xn, wqkv, means):
    qkv = dot(xn, wqkv)
    raw_q, raw_k = qkv[:, :D], qkv[:, D : 2 * D]
    rq, rk = head_scale(raw_q, means), head_scale(raw_k, means)
    qs = (raw_q * (rq * QSCALE)).astype(BF16)
    kn = (raw_k * rk).astype(BF16)
    return qs, kn, qkv[:, 2 * D :].astype(BF16), rq, rk


def head_masks(rows):
    lane = div(iota((rows, D), 1), HD)
    return [lane == h for h in range(HEADS)]


def stack_heads(x, masks):
    zero = jnp.zeros_like(x)
    return jnp.concatenate([jnp.where(m, x, zero) for m in masks], axis=0)


def time_diag():
    row, col = iota((BLK, HEADS * BLK), 0), iota((BLK, HEADS * BLK), 1)
    return jnp.where(div(row, L) == div(col & (BLK - 1), L), 1.0, 0.0).astype(F32)


def head_columns():
    return [slice(h * BLK, (h + 1) * BLK) for h in range(HEADS)]


def stack_product(xts, parts):
    out = []
    for xt, p in zip(xts, parts):
        heads = [dot(xt[h * HD : (h + 1) * HD], p[:, c]) for h, c in enumerate(head_columns())]
        out.append(jnp.concatenate(heads, axis=0).T)
    return out


def softmax_columns(es):
    return [e * (1.0 / jnp.sum(e, axis=0, keepdims=True)) for e in es]


def score_grads(ps, dps):
    ts = [p * dp for p, dp in zip(ps, dps)]
    return [
        (t - p * jnp.sum(t, axis=0, keepdims=True)).astype(BF16) for t, p in zip(ts, ps)
    ]


def split(x, size=BLK):
    return [x[i : i + size] for i in range(0, x.shape[0], size)]


def join(parts):
    return jnp.concatenate(parts, axis=0)


def load_wqkv(w_ref):
    return jnp.concatenate([w_ref[0], w_ref[1], w_ref[2]], axis=1)


def loop(size, body):
    def step(i, carry):
        body(i, pl.ds(pl.multiple_of(i * size, size), size))
        return carry

    lax.fori_loop(0, ROWS // size, step, 0)


def copies(src, dst, sems, size):
    return [
        pltpu.make_async_copy(
            src.at[pl.ds(i * size, size)], dst.at[pl.ds(i * size, size)], sems.at[i]
        )
        for i in range(ROWS // size)
    ]


def kept_copies(srcs, dsts, sems, size):
    out = []
    for i in range(ROWS // size):
        step = []
        for n, (src, dst) in enumerate(zip(srcs, dsts)):
            rows = size // BLK if len(src.shape) == 3 else size
            at = pl.ds(i * rows, rows)
            step.append(pltpu.make_async_copy(src.at[at], dst.at[at], sems.at[n, i]))
        out.append(step)
    return out


A_STEP = 1024


def time_forward_kernel(x_hbm, w_hbm, out_hbm, x_ref, w_ref, out_ref, w_sem, in_sem, out_sem):
    w_in = pltpu.make_async_copy(w_hbm, w_ref, w_sem)
    x_in = copies(x_hbm, x_ref, in_sem, A_STEP)
    x_in[0].start()
    w_in.start()
    for c in x_in[1:]:
        c.start()
    means, swap = head_mean_matrix(), swap_matrix()
    masks = head_masks(BLK)
    diag = time_diag()
    ones = jnp.where(
        div(iota((HEADS * BLK, D), 0), BLK) == div(iota((HEADS * BLK, D), 1), HD), 1.0, 0.0
    ).astype(BF16)
    chans = A_STEP // L
    outs = []
    for i in range(ROWS // A_STEP):
        x_in[i].wait()
        if i == 0:
            w_in.wait()
            wqkv = load_wqkv(w_ref)
            wo = w_ref[3]
        x = x_ref[i * A_STEP : (i + 1) * A_STEP, :].astype(F32)
        xn = (x * rms_scale(x)).astype(BF16)
        qs, kn, v, _, _ = project(xn, wqkv, means)
        es = [
            (jnp.exp2(dot_rt(q, stack_heads(k, masks))) * diag).astype(BF16)
            for q, k in zip(split(qs), split(kn))
        ]
        dens = [dot(e, ones) for e in es]
        os = [dot(e, stack_heads(u, masks)) for e, u in zip(es, split(v))]
        mixed = join([(o * (1.0 / den)).astype(BF16) for o, den in zip(os, dens)])
        stream = (x + dot(mixed, wo)).astype(BF16)
        for j, part in enumerate(split(stream, SQ)):
            at = i * chans + j * L
            out_ref[:, at : at + L, :] = dot(swap, part).astype(BF16).reshape(L, L, D)
        at = pl.ds(i * chans, chans)
        c = pltpu.make_async_copy(out_ref.at[:, at], out_hbm.at[:, at], out_sem.at[i])
        c.start()
        outs.append(c)
    for c in outs:
        c.wait()


PREP_STEP = 512


def prepare_kernel(x_ref, w_ref, *refs):
    outs, (xn_ref, qs_ref, kn_ref, v_ref, rq_ref, rk_ref, p_ref, mixed_ref), sems = (
        refs[:8], refs[8:16], refs[16],
    )
    means = head_mean_matrix()
    masks = head_masks(BLK)
    diag = time_diag()
    wqkv = load_wqkv(w_ref)
    groups = PREP_STEP // BLK
    moves = kept_copies(refs[8:16], outs, sems, PREP_STEP)
    for i in range(ROWS // PREP_STEP):
        at = slice(i * PREP_STEP, (i + 1) * PREP_STEP)
        x = x_ref[at, :].astype(F32)
        xn = (x * rms_scale(x)).astype(BF16)
        qs, kn, v, rq, rk = project(xn, wqkv, means)
        xn_ref[at, :] = xn
        qs_ref[at, :] = qs
        kn_ref[at, :] = kn
        v_ref[at, :] = v
        rq_ref[at, :] = rq.astype(BF16)
        rk_ref[at, :] = rk.astype(BF16)
        es = [
            jnp.exp2(dot_rt(k, stack_heads(q, masks))) * diag
            for q, k in zip(split(qs), split(kn))
        ]
        pbs = [p.astype(BF16) for p in softmax_columns(es)]
        p_ref[i * groups : (i + 1) * groups] = jnp.stack(pbs)
        os = stack_product([u.T for u in split(v)], pbs)
        mixed_ref[at, :] = join(os).astype(BF16)
        for c in moves[i]:
            c.start()
    for step in moves:
        for c in step:
            c.wait()


def head_back(r, y, g, means, scale):
    yf = y.astype(F32)
    m = dot((yf * g).astype(BF16), means)
    return r * (g - yf * (m * scale))


def query_back(rq, qs, dq, means):
    return head_back(rq, qs, dq, means, 1.0 / (QSCALE * QSCALE)).astype(BF16)


def key_back(rk, kn, dk, means):
    return head_back(rk * LN2, kn, dk, means, 1.0).astype(BF16)


def rms_back(x, r, ng):
    xh = x * r
    return r * (ng - xh * jnp.mean(xh * ng, axis=-1, keepdims=True))


def write_grads(grads_ref, acc, acc_o):
    for j in range(4):
        whole = (acc[:, j * D : (j + 1) * D] if j < 3 else acc_o[...]).reshape(16, 2, 8, D)
        for half in range(2):
            grads_ref[half, :, j] = whole[:, half].astype(BF16)


T_STEP = 512


def time_backward_kernel(sg_ref, w_hbm, *refs):
    kept_hbm, back_hbm, grads_ref = refs[:8], refs[8], refs[9]
    w_ref, kept, back_ref, acc, acc_o = refs[10], refs[11:19], refs[19], refs[20], refs[21]
    w_sem, in_sem, out_sem = refs[22:]
    xn_ref, qs_ref, kn_ref, v_ref, rq_ref, rk_ref, p_ref, mixed_ref = kept
    w_in = pltpu.make_async_copy(w_hbm, w_ref, w_sem)
    w_in.start()
    moves = kept_copies(kept_hbm, kept, in_sem, T_STEP)
    for step in moves:
        for c in step:
            c.start()
    back_out = copies(back_ref, back_hbm, out_sem, T_STEP)
    means, swap = head_mean_matrix(), swap_matrix()
    masks = head_masks(BLK)
    groups, chans = T_STEP // BLK, T_STEP // L
    w_in.wait()
    wo = w_ref[...]
    for i in range(ROWS // T_STEP):
        at = slice(i * T_STEP, (i + 1) * T_STEP)
        sg = []
        for j in range(T_STEP // SQ):
            part = sg_ref[:, i * chans + j * L : i * chans + (j + 1) * L, :]
            sg.append(dot(swap, part.reshape(SQ, D)).astype(BF16))
        sg = join(sg)
        do = dot_rt(sg, wo).astype(BF16)
        for c in moves[i]:
            c.wait()
        qs, kn = qs_ref[at, :], kn_ref[at, :]
        pbs = [p_ref[i * groups + g] for g in range(groups)]
        dosts = [stack_heads(d, masks) for d in split(do)]
        dps = [dot_rt(v, d) for v, d in zip(split(v_ref[at, :]), dosts)]
        dss = score_grads([p.astype(F32) for p in pbs], dps)
        vb = join([dot(p, d).astype(BF16) for p, d in zip(pbs, dosts)])
        dk = join([dot(ds, stack_heads(q, masks)) for ds, q in zip(dss, split(qs))])
        dq = join(stack_product([k.T for k in split(kn)], dss))
        qb = query_back(rq_ref[at, :].astype(F32) * 0.25, qs, dq, means)
        kb = key_back(rk_ref[at, :].astype(F32), kn, dk, means)
        back = jnp.concatenate([qb, kb, vb], axis=1)
        back_ref[at, :] = back
        back_out[i].start()
        part, part_o = dot_lt(xn_ref[at, :], back), dot_lt(mixed_ref[at, :], sg)
        acc[...] = part if i == 0 else acc[...] + part
        acc_o[...] = part_o if i == 0 else acc_o[...] + part_o
    write_grads(grads_ref, acc, acc_o)
    for c in back_out:
        c.wait()


S_STEP = 512


def series_grad_kernel(x_ref, sg_ref, back_ref, w_ref, out_ref):
    swap = swap_matrix()
    wqkv = load_wqkv(w_ref)
    chans = S_STEP // L

    def body(i, at):
        x = x_ref[at, :].astype(F32)
        sg = []
        for j in range(S_STEP // SQ):
            part = sg_ref[:, pl.ds(pl.multiple_of(i * chans + j * L, L), L), :]
            sg.append(dot(swap, part.reshape(SQ, D)))
        ng = dot_rt(back_ref[at, :], wqkv)
        out_ref[at, :] = (join(sg) + rms_back(x, rms_scale(x), ng)).astype(BF16)

    loop(S_STEP, body)


C_STEP = 512


def channel_kernel(
    nb_ref, x_ref, up_hbm, w_hbm, sg_hbm, back_hbm, mixed_hbm,
    up_ref, w_ref, do_ref, up_sem, w_sem, sg_s, back_s, mixed_s, qs_s, kn_s, v_s, kt_s, vt_s, rq_s, rk_s, dq_s, dk_s, dv_s,
    sg_sem, back_sem, mixed_sem,
):
    w_in = pltpu.make_async_copy(w_hbm, w_ref, w_sem)
    w_in.start()
    up_in = pltpu.make_async_copy(up_hbm, up_ref, up_sem)
    up_in.start()
    means = head_mean_matrix()
    masks = head_masks(BLK)
    w_in.wait()
    wqkv = load_wqkv(w_ref)
    wo = w_ref[3]
    up_in.wait()

    def first(i, at):
        do_ref[at, :] = dot_rt(up_ref[at, :], wo).astype(BF16)
        x = x_ref[at, :].astype(F32)
        xn = (x * rms_scale(x)).astype(BF16)
        qs, kn, v, rq_s[at, :], rk_s[at, :] = project(xn, wqkv, means)
        qs_s[at, :] = qs
        kn_s[at, :] = kn
        v_s[at, :] = v
        kt_s[:, at] = kn.T
        vt_s[:, at] = v.T
        dk_s[at, :] = jnp.zeros((C_STEP, D), F32)
        dv_s[at, :] = jnp.zeros((C_STEP, D), F32)

    loop(C_STEP, first)

    def attend(i, carry):
        bs = [i * GROUPS + g for g in range(GROUPS)]
        ats = [pl.ds(pl.multiple_of(b * BLK, BLK), BLK) for b in bs]
        nears = [
            [pl.ds(pl.multiple_of(nb_ref[b, j] * BLK, BLK), BLK) for j in range(NBR)] for b in bs
        ]
        qsts = [stack_heads(qs_s[at, :], masks) for at in ats]
        es = [
            jnp.exp2(dot_rt(join([kn_s[n, :] for n in near]), q))
            for near, q in zip(nears, qsts)
        ]
        dosts = [stack_heads(do_ref[at, :], masks) for at in ats]
        dps = [dot_rt(join([v_s[n, :] for n in near]), d) for near, d in zip(nears, dosts)]
        ps = softmax_columns(es)
        pbs = [p.astype(BF16) for p in ps]
        dss = score_grads(ps, dps)
        dvs = [dot(p, d) for p, d in zip(pbs, dosts)]
        os = stack_product(
            [jnp.concatenate([vt_s[:, n] for n in near], axis=1) for near in nears], pbs
        )
        dks = [dot(ds, q) for ds, q in zip(dss, qsts)]
        dqs = stack_product(
            [jnp.concatenate([kt_s[:, n] for n in near], axis=1) for near in nears], dss
        )
        for at, o, dq in zip(ats, os, dqs):
            mixed_s[at, :] = o.astype(BF16)
            dq_s[at, :] = dq
        for near, dk, dv in zip(nears, dks, dvs):
            for n, k_part, v_part in zip(near, split(dk), split(dv)):
                dk_s[n, :] += k_part
                dv_s[n, :] += v_part
        return carry

    lax.fori_loop(0, ROWS // BLK // GROUPS, attend, 0)

    mixed_out = pltpu.make_async_copy(mixed_s, mixed_hbm, mixed_sem)
    mixed_out.start()
    sg_out = copies(sg_s, sg_hbm, sg_sem, C_STEP)
    back_out = copies(back_s, back_hbm, back_sem, C_STEP)
    for i in range(ROWS // C_STEP):
        at = slice(i * C_STEP, (i + 1) * C_STEP)
        x = x_ref[at, :].astype(F32)
        r = rms_scale(x)
        qb = query_back(rq_s[at, :] * 0.25, qs_s[at, :], dq_s[at, :], means)
        kb = key_back(rk_s[at, :], kn_s[at, :], dk_s[at, :], means)
        back = jnp.concatenate([qb, kb, dv_s[at, :].astype(BF16)], axis=1)
        back_s[at, :] = back
        back_out[i].start()
        dx = rms_back(x, r, dot_rt(back, wqkv))
        sg_s[at, :] = (up_ref[at, :].astype(F32) + dx).astype(BF16)
        sg_out[i].start()
    mixed_out.wait()
    for c in back_out + sg_out:
        c.wait()


G_STEP = 512


def channel_grads_kernel(x_ref, up_ref, back_ref, mixed_ref, w_ref, out_ref, grads_ref, acc, acc_o):
    wo = w_ref[3]
    acc[...] = jnp.zeros_like(acc)
    acc_o[...] = jnp.zeros_like(acc_o)

    def body(i, at):
        x = x_ref[at, :].astype(F32)
        xn = (x * rms_scale(x)).astype(BF16)
        mixed = mixed_ref[at, :]
        out_ref[at, :] = (x + dot(mixed, wo)).astype(BF16)
        acc[...] += dot_lt(xn, back_ref[at, :])
        acc_o[...] += dot_lt(mixed, up_ref[at, :])

    loop(G_STEP, body)
    write_grads(grads_ref, acc, acc_o)


VM = pl.BlockSpec(memory_space=pltpu.VMEM)
HB = pl.BlockSpec(memory_space=pltpu.HBM)
SM = pl.BlockSpec(memory_space=pltpu.SMEM)
DMA = pltpu.SemaphoreType.DMA


def shape(dims, dtype=BF16):
    return jax.ShapeDtypeStruct(dims, dtype)


def vm(dims, dtype=BF16):
    return pltpu.VMEM(dims, dtype)


ROW = (ROWS, D)
GRADS = (2, 16, 4, 8, D)


def call(kernel, name, mib, outs, ins, out_specs, args, scratch=(), flops=0):
    args = [
        pltpu.with_memory_space_constraint(a, pltpu.HBM) if spec is HB else a
        for a, spec in zip(args, ins)
    ]
    return pl.pallas_call(
        kernel,
        out_shape=[
            pltpu.HBM(o.shape, o.dtype) if spec is HB else o for o, spec in zip(outs, out_specs)
        ],
        in_specs=ins,
        out_specs=out_specs,
        scratch_shapes=scratch,
        compiler_params=pltpu.CompilerParams(vmem_limit_bytes=mib << 20),
        cost_estimate=pl.CostEstimate(
            flops=flops, bytes_accessed=8 << 20, transcendentals=1 << 20
        ),
        name=name,
    )(*args)


def time_forward(x, w):
    return call(
        time_forward_kernel, "time_forward", 24, [shape((L, CH, D))], [HB, HB], [HB], (x, w),
        [vm(ROW), vm((4, D, D)), vm((L, CH, D)), DMA, DMA((2,)), DMA((2,))],
        flops=2 * 10**9,
    )[0]


def prepare(x, w):
    names = [shape(ROW)] * 6 + [shape((ROWS // BLK, BLK, HEADS * BLK)), shape(ROW)]
    return call(
        prepare_kernel, "prepare", 28, names, [VM] * 2, [HB] * 8, (x, w),
        [vm(o.shape) for o in names] + [DMA((8, ROWS // PREP_STEP))],
        flops=3 * 10**9,
    )


def channel(nb, x, up, w):
    return call(
        channel_kernel, "channel", 36,
        [shape(ROW), shape((ROWS, 3 * D)), shape(ROW)],
        [SM, VM, HB, HB], [HB] * 3, (nb, x, up, w),
        [vm(ROW), vm((4, D, D)), vm(ROW), DMA, DMA]
        + [vm(ROW), vm((ROWS, 3 * D)), vm(ROW), vm(ROW), vm(ROW), vm(ROW)]
        + [vm((D, ROWS))] * 2 + [vm(ROW, F32)] * 5 + [DMA((4,)), DMA((4,)), DMA],
        flops=8 * 10**9,
    )


def channel_grads(x, up, back, mixed, w):
    return call(
        channel_grads_kernel, "channel_grads", 20, [shape(ROW), shape(GRADS)],
        [VM] * 5, [VM] * 2, (x, up, back, mixed, w),
        [vm((D, 3 * D), F32), vm((D, D), F32)], flops=2 * 10**9,
    )


def time_backward(sg, kept, w):
    return call(
        time_backward_kernel, "time_backward", 30, [shape((ROWS, 3 * D)), shape(GRADS)],
        [VM] + [HB] * 9, [HB, VM], (sg, w[3]) + tuple(kept),
        [vm((D, D))] + [vm(k.shape) for k in kept]
        + [vm((ROWS, 3 * D)), vm((D, 3 * D), F32), vm((D, D), F32)]
        + [DMA, DMA((8, ROWS // T_STEP)), DMA((ROWS // T_STEP,))],
        flops=4 * 10**9,
    )


def series_gradient(x, sg, back, w):
    return call(
        series_grad_kernel, "series_grad", 20, [shape(ROW)], [VM] * 4, [VM], (x, sg, back, w),
        flops=10**9,
    )[0]


def exchange(x, axis, groups=None):
    return lax.all_to_all(
        x, axis, split_axis=0, concat_axis=0, tiled=True, axis_index_groups=groups
    )


def other_core(x):
    return lax.ppermute(x, "dp", [(i, i ^ 1) for i in range(16)])


def add_cores(parts, core):
    mine = lax.dynamic_index_in_dim(parts, core, 0, keepdims=False)
    theirs = lax.dynamic_index_in_dim(other_core(parts), core, 0, keepdims=False)
    return (mine.astype(F32) + theirs.astype(F32)).astype(BF16)


CHIPS = [[i for i in range(16) if i % 2 == c] for c in range(2)]


def reduce_grads(halves, core, beside):
    rows = exchange(halves, "mp")
    halves_first = lambda a: lax.optimization_barrier((a, halves))[0]
    other = beside(halves_first)
    rows, other = lax.optimization_barrier((rows, other))
    mine = jnp.sum(rows.astype(F32), axis=0).astype(BF16)
    every = exchange(jnp.broadcast_to(mine[None], (8,) + mine.shape), "dp", CHIPS)
    total = jnp.sum(every.astype(F32), axis=0).astype(BF16)
    theirs = other_core(total)
    low = jnp.where(core == 0, total, theirs)
    high = jnp.where(core == 0, theirs, total)
    return jnp.concatenate([low, high], axis=1).astype(F32) * (1.0 / 16), other


def shards(series, upstream_grad, time_weights, channel_weights, neighbors):
    core = lax.axis_index("dp") & 1
    x = series.reshape(ROWS, D)
    up = upstream_grad.reshape(ROWS, D)
    stream = exchange(time_forward(x, time_weights), "mp").reshape(ROWS, D)
    sg, back, mixed = channel(neighbors, stream, up, channel_weights)
    x, sg = lax.optimization_barrier((x, sg))
    returned = exchange(sg.reshape(16, CH, D), "mp")
    out, channel_parts = channel_grads(stream, up, back, mixed, channel_weights)
    channel_half = add_cores(channel_parts, core)
    kept = prepare(x, time_weights)
    returned, channel_half, kept = lax.optimization_barrier((returned, channel_half, kept))
    time_back, time_parts = time_backward(returned, kept, time_weights)
    halves = jnp.concatenate([channel_half, add_cores(time_parts, core)], axis=1)
    sums, series_grad = reduce_grads(
        halves, core, lambda gate: series_gradient(x, returned, gate(time_back), time_weights)
    )
    return (
        out.reshape(1, ROWS, 1, D),
        series_grad.reshape(1, CH, L, D),
        sums[4:],
        sums[:4],
    )


def solution(mesh):
    placed = (P("dp", "mp", None, None), P("dp", None, "mp", None), P(), P(), P())
    return jax.shard_map(
        shards,
        mesh=mesh,
        in_specs=placed,
        out_specs=(
            P("dp", None, "mp", None),
            P("dp", "mp", None, None),
            P(None, "mp", None),
            P(None, "mp", None),
        ),
        check_vma=False,
    )
```

```python
import jax
import jax.numpy as jnp
from jax import lax
from jax.experimental import pallas as pl
from jax.experimental.pallas import tpu as pltpu
from jax.sharding import PartitionSpec as P

HEADS = 4
D = 256
HD = D // HEADS
L = 16
CH = 128
BLK = 128
NBR = 3
ROWS = 2048
SQ = 256
GROUPS = 4
EPS = 1e-06
LOG2E = 1.4426950408889634
LN2 = 0.6931471805599453
QSCALE = 0.25 * LOG2E
F32 = jnp.float32
BF16 = jnp.bfloat16


def dot(a, b):
    return lax.dot_general(a, b, (((1,), (0,)), ((), ())), preferred_element_type=F32)


def dot_rt(a, b):
    return lax.dot_general(a, b, (((1,), (1,)), ((), ())), preferred_element_type=F32)


def dot_lt(a, b):
    return lax.dot_general(a, b, (((0,), (0,)), ((), ())), preferred_element_type=F32)


def iota(shape, dim):
    return lax.broadcasted_iota(jnp.int32, shape, dim)


def div(a, n):
    return lax.shift_right_logical(a, jnp.int32(n.bit_length() - 1))


def head_mean_matrix():
    same = div(iota((D, D), 0), HD) == div(iota((D, D), 1), HD)
    return jnp.where(same, 1.0 / HD, 0.0).astype(BF16)


def swap_matrix():
    row, col = iota((D, D), 0), iota((D, D), 1)
    same = (div(row, L) == (col & (L - 1))) & ((row & (L - 1)) == div(col, L))
    return jnp.where(same, 1.0, 0.0).astype(BF16)


def rms_scale(x):
    return lax.rsqrt(jnp.mean(x * x, axis=-1, keepdims=True) + EPS)


def head_scale(raw, means):
    return lax.rsqrt(dot((raw * raw).astype(BF16), means) + EPS)


def project(xn, wqkv, means):
    qkv = dot(xn, wqkv)
    raw_q, raw_k = qkv[:, :D], qkv[:, D : 2 * D]
    rq, rk = head_scale(raw_q, means), head_scale(raw_k, means)
    qs = (raw_q * (rq * QSCALE)).astype(BF16)
    kn = (raw_k * rk).astype(BF16)
    return qs, kn, qkv[:, 2 * D :].astype(BF16), rq, rk


def head_masks(rows):
    lane = div(iota((rows, D), 1), HD)
    return [lane == h for h in range(HEADS)]


def stack_heads(x, masks):
    zero = jnp.zeros_like(x)
    return jnp.concatenate([jnp.where(m, x, zero) for m in masks], axis=0)


def time_diag():
    row, col = iota((BLK, HEADS * BLK), 0), iota((BLK, HEADS * BLK), 1)
    return jnp.where(div(row, L) == div(col & (BLK - 1), L), 1.0, 0.0).astype(F32)


def head_columns():
    return [slice(h * BLK, (h + 1) * BLK) for h in range(HEADS)]


def stack_product(xts, parts):
    out = []
    for xt, p in zip(xts, parts):
        heads = [dot(xt[h * HD : (h + 1) * HD], p[:, c]) for h, c in enumerate(head_columns())]
        out.append(jnp.concatenate(heads, axis=0).T)
    return out


def softmax_columns(es):
    return [e * (1.0 / jnp.sum(e, axis=0, keepdims=True)) for e in es]


def score_grads(ps, dps):
    ts = [p * dp for p, dp in zip(ps, dps)]
    return [
        (t - p * jnp.sum(t, axis=0, keepdims=True)).astype(BF16) for t, p in zip(ts, ps)
    ]


def split(x, size=BLK):
    return [x[i : i + size] for i in range(0, x.shape[0], size)]


def join(parts):
    return jnp.concatenate(parts, axis=0)


def load_wqkv(w_ref):
    return jnp.concatenate([w_ref[0], w_ref[1], w_ref[2]], axis=1)


def loop(size, body):
    def step(i, carry):
        body(i, pl.ds(pl.multiple_of(i * size, size), size))
        return carry

    lax.fori_loop(0, ROWS // size, step, 0)


def copies(src, dst, sems, size):
    return [
        pltpu.make_async_copy(
            src.at[pl.ds(i * size, size)], dst.at[pl.ds(i * size, size)], sems.at[i]
        )
        for i in range(ROWS // size)
    ]


def kept_copies(srcs, dsts, sems, size):
    out = []
    for i in range(ROWS // size):
        step = []
        for n, (src, dst) in enumerate(zip(srcs, dsts)):
            rows = size // BLK if len(src.shape) == 3 else size
            at = (slice(None), pl.ds(i * rows, rows)) if src.shape[0] == D else pl.ds(i * rows, rows)
            step.append(pltpu.make_async_copy(src.at[at], dst.at[at], sems.at[n, i]))
        out.append(step)
    return out


A_STEP = 1024


def time_forward_kernel(x_hbm, w_hbm, out_hbm, x_ref, w_ref, out_ref, w_sem, in_sem, out_sem):
    w_in = pltpu.make_async_copy(w_hbm, w_ref, w_sem)
    x_in = copies(x_hbm, x_ref, in_sem, A_STEP)
    x_in[0].start()
    w_in.start()
    for c in x_in[1:]:
        c.start()
    means, swap = head_mean_matrix(), swap_matrix()
    masks = head_masks(BLK)
    diag = time_diag()
    chans = A_STEP // L
    outs = []
    for i in range(ROWS // A_STEP):
        x_in[i].wait()
        if i == 0:
            w_in.wait()
            wqkv = load_wqkv(w_ref)
            wo = w_ref[3]
        x = x_ref[i * A_STEP : (i + 1) * A_STEP, :].astype(F32)
        xn = (x * rms_scale(x)).astype(BF16)
        qs, kn, v, _, _ = project(xn, wqkv, means)
        es = [
            jnp.exp2(dot_rt(k, stack_heads(q, masks))) * diag
            for q, k in zip(split(qs), split(kn))
        ]
        pbs = [p.astype(BF16) for p in softmax_columns(es)]
        mixed = join(stack_product([u.T for u in split(v)], pbs)).astype(BF16)
        stream = (x + dot(mixed, wo)).astype(BF16)
        for j, part in enumerate(split(stream, SQ)):
            at = i * chans + j * L
            out_ref[:, at : at + L, :] = dot(swap, part).astype(BF16).reshape(L, L, D)
        at = pl.ds(i * chans, chans)
        c = pltpu.make_async_copy(out_ref.at[:, at], out_hbm.at[:, at], out_sem.at[i])
        c.start()
        outs.append(c)
    for c in outs:
        c.wait()


PREP_STEP = 512


def prepare_kernel(x_ref, w_ref, v_ref, *refs):
    outs, (xt_ref, p_ref, qs_ref, kn_ref, rq_ref, rk_ref, mt_ref), sems = (
        refs[:7], refs[7:14], refs[14],
    )
    means = head_mean_matrix()
    masks = head_masks(BLK)
    diag = time_diag()
    wqkv = load_wqkv(w_ref)
    groups = PREP_STEP // BLK
    moves = kept_copies(refs[7:14], outs, sems, PREP_STEP)
    for i in range(ROWS // PREP_STEP):
        at = slice(i * PREP_STEP, (i + 1) * PREP_STEP)
        x = x_ref[at, :].astype(F32)
        xn = (x * rms_scale(x)).astype(BF16)
        qs, kn, v, rq, rk = project(xn, wqkv, means)
        xt_ref[:, at] = xn.T
        qs_ref[at, :] = qs
        kn_ref[at, :] = kn
        v_ref[at, :] = v
        rq_ref[at, :] = rq.astype(BF16)
        rk_ref[at, :] = rk.astype(BF16)
        es = [
            jnp.exp2(dot_rt(k, stack_heads(q, masks))) * diag
            for q, k in zip(split(qs), split(kn))
        ]
        pbs = [p.astype(BF16) for p in softmax_columns(es)]
        p_ref[i * groups : (i + 1) * groups] = jnp.stack(pbs)
        os = stack_product([u.T for u in split(v)], pbs)
        mt_ref[:, at] = join(os).astype(BF16).T
        for c in moves[i]:
            c.start()
    for step in moves:
        for c in step:
            c.wait()


def head_back(r, y, g, means, scale):
    yf = y.astype(F32)
    m = dot((yf * g).astype(BF16), means)
    return r * (g - yf * (m * scale))


def query_back(rq, qs, dq, means):
    return head_back(rq, qs, dq, means, 1.0 / (QSCALE * QSCALE)).astype(BF16)


def key_back(rk, kn, dk, means):
    return head_back(rk * LN2, kn, dk, means, 1.0).astype(BF16)


def rms_back(x, r, ng):
    xh = x * r
    return r * (ng - xh * jnp.mean(xh * ng, axis=-1, keepdims=True))


def write_grads(grads_ref, acc, acc_o):
    for j in range(4):
        whole = (acc[:, j * D : (j + 1) * D] if j < 3 else acc_o[...]).reshape(16, 2, 8, D)
        for half in range(2):
            grads_ref[half, :, j] = whole[:, half].astype(BF16)


T_STEP = 1024


def time_backward_kernel(sg_ref, w_hbm, v_ref, *refs):
    kept_hbm, back_hbm, grads_ref = refs[:7], refs[7], refs[8]
    w_ref, kept, back_ref, acc, acc_o = refs[9], refs[10:17], refs[17], refs[18], refs[19]
    w_sem, in_sem, out_sem = refs[20:]
    xt_ref, p_ref, qs_ref, kn_ref, rq_ref, rk_ref, mt_ref = kept
    w_in = pltpu.make_async_copy(w_hbm, w_ref, w_sem)
    w_in.start()
    moves = kept_copies(kept_hbm, kept, in_sem, T_STEP)
    for c in moves[0]:
        c.start()
    back_out = copies(back_ref, back_hbm, out_sem, T_STEP)
    means, swap = head_mean_matrix(), swap_matrix()
    masks = head_masks(BLK)
    groups, chans = T_STEP // BLK, T_STEP // L
    w_in.wait()
    wo = w_ref[...]
    for i in range(ROWS // T_STEP):
        at = slice(i * T_STEP, (i + 1) * T_STEP)
        sg = []
        for j in range(T_STEP // SQ):
            part = sg_ref[:, i * chans + j * L : i * chans + (j + 1) * L, :]
            sg.append(dot(swap, part.reshape(SQ, D)).astype(BF16))
        sg = join(sg)
        do = dot_rt(sg, wo).astype(BF16)
        for c in moves[i]:
            c.wait()
        for c in moves[i + 1] if i + 1 < len(moves) else []:
            c.start()
        qs, kn = qs_ref[at, :], kn_ref[at, :]
        pbs = [p_ref[i * groups + g] for g in range(groups)]
        dosts = [stack_heads(d, masks) for d in split(do)]
        dps = [dot_rt(v, d) for v, d in zip(split(v_ref[at, :]), dosts)]
        dss = score_grads([p.astype(F32) for p in pbs], dps)
        vb = join([dot(p, d).astype(BF16) for p, d in zip(pbs, dosts)])
        dk = join([dot(ds, stack_heads(q, masks)) for ds, q in zip(dss, split(qs))])
        dq = join(stack_product([k.T for k in split(kn)], dss))
        qb = query_back(rq_ref[at, :].astype(F32) * 0.25, qs, dq, means)
        kb = key_back(rk_ref[at, :].astype(F32), kn, dk, means)
        back = jnp.concatenate([qb, kb, vb], axis=1)
        back_ref[at, :] = back
        back_out[i].start()
        part, part_o = dot(xt_ref[:, at], back), dot(mt_ref[:, at], sg)
        acc[...] = part if i == 0 else acc[...] + part
        acc_o[...] = part_o if i == 0 else acc_o[...] + part_o
    write_grads(grads_ref, acc, acc_o)
    for c in back_out:
        c.wait()


S_STEP = 512


def series_grad_kernel(x_ref, sg_ref, back_ref, w_ref, out_ref):
    swap = swap_matrix()
    wqkv = load_wqkv(w_ref)
    chans = S_STEP // L

    def body(i, at):
        x = x_ref[at, :].astype(F32)
        sg = []
        for j in range(S_STEP // SQ):
            part = sg_ref[:, pl.ds(pl.multiple_of(i * chans + j * L, L), L), :]
            sg.append(dot(swap, part.reshape(SQ, D)))
        ng = dot_rt(back_ref[at, :], wqkv)
        out_ref[at, :] = (join(sg) + rms_back(x, rms_scale(x), ng)).astype(BF16)

    loop(S_STEP, body)


C_STEP = 1024


def channel_kernel(
    nb_ref, x_ref, up_hbm, w_hbm, sg_hbm, back_hbm, mixed_hbm,
    up_ref, w_ref, up_sem, w_sem, sg_s, back_s, mixed_s, qs_s, kn_s, v_s, kt_s, vt_s, rq_s, rk_s, dq_s, dk_s, dv_s,
    sg_sem, back_sem, mixed_sem,
):
    w_in = pltpu.make_async_copy(w_hbm, w_ref, w_sem)
    w_in.start()
    up_in = pltpu.make_async_copy(up_hbm, up_ref, up_sem)
    up_in.start()
    means = head_mean_matrix()
    masks = head_masks(BLK)
    w_in.wait()
    wqkv = load_wqkv(w_ref)
    wo = w_ref[3]

    def first(i, at):
        x = x_ref[at, :].astype(F32)
        xn = (x * rms_scale(x)).astype(BF16)
        qs, kn, v, rq, rk = project(xn, wqkv, means)
        rq_s[at, :] = rq.astype(BF16)
        rk_s[at, :] = rk.astype(BF16)
        qs_s[at, :] = qs
        kn_s[at, :] = kn
        v_s[at, :] = v
        kt_s[:, at] = kn.T
        vt_s[:, at] = v.T
        dk_s[at, :] = jnp.zeros((C_STEP, D), F32)
        dv_s[at, :] = jnp.zeros((C_STEP, D), F32)

    loop(C_STEP, first)
    up_in.wait()

    span = GROUPS * BLK

    def attend(i, carry):
        bs = [i * GROUPS + g for g in range(GROUPS)]
        ats = [pl.ds(pl.multiple_of(b * BLK, BLK), BLK) for b in bs]
        nears = [
            [pl.ds(pl.multiple_of(nb_ref[b, j] * BLK, BLK), BLK) for j in range(NBR)] for b in bs
        ]
        qsts = [stack_heads(qs_s[at, :], masks) for at in ats]
        es = [
            jnp.exp2(dot_rt(join([kn_s[n, :] for n in near]), q))
            for near, q in zip(nears, qsts)
        ]
        do = dot_rt(up_ref[pl.ds(pl.multiple_of(i * span, span), span), :], wo).astype(BF16)
        dosts = [stack_heads(d, masks) for d in split(do)]
        dps = [dot_rt(join([v_s[n, :] for n in near]), d) for near, d in zip(nears, dosts)]
        ps = softmax_columns(es)
        pbs = [p.astype(BF16) for p in ps]
        dss = score_grads(ps, dps)
        dvs = [dot(p, d) for p, d in zip(pbs, dosts)]
        os = stack_product(
            [jnp.concatenate([vt_s[:, n] for n in near], axis=1) for near in nears], pbs
        )
        dks = [dot(ds, q) for ds, q in zip(dss, qsts)]
        dqs = stack_product(
            [jnp.concatenate([kt_s[:, n] for n in near], axis=1) for near in nears], dss
        )
        for at, o, dq in zip(ats, os, dqs):
            mixed_s[at, :] = o.astype(BF16)
            dq_s[at, :] = dq
        for near, dk, dv in zip(nears, dks, dvs):
            for n, k_part, v_part in zip(near, split(dk), split(dv)):
                dk_s[n, :] += k_part
                dv_s[n, :] += v_part
        return carry

    lax.fori_loop(0, ROWS // BLK // GROUPS, attend, 0)

    mixed_out = pltpu.make_async_copy(mixed_s, mixed_hbm, mixed_sem)
    mixed_out.start()
    sg_out = copies(sg_s, sg_hbm, sg_sem, C_STEP)
    back_out = copies(back_s, back_hbm, back_sem, C_STEP)
    for i in range(ROWS // C_STEP):
        at = slice(i * C_STEP, (i + 1) * C_STEP)
        x = x_ref[at, :].astype(F32)
        r = rms_scale(x)
        qb = query_back(rq_s[at, :].astype(F32) * 0.25, qs_s[at, :], dq_s[at, :], means)
        kb = key_back(rk_s[at, :].astype(F32), kn_s[at, :], dk_s[at, :], means)
        back = jnp.concatenate([qb, kb, dv_s[at, :].astype(BF16)], axis=1)
        back_s[at, :] = back
        back_out[i].start()
        dx = rms_back(x, r, dot_rt(back, wqkv))
        sg_s[at, :] = (up_ref[at, :].astype(F32) + dx).astype(BF16)
        sg_out[i].start()
    mixed_out.wait()
    for c in back_out + sg_out:
        c.wait()


G_STEP = 512


def channel_grads_kernel(x_ref, up_ref, back_ref, mixed_ref, w_ref, out_ref, grads_ref, acc, acc_o):
    wo = w_ref[3]
    acc[...] = jnp.zeros_like(acc)
    acc_o[...] = jnp.zeros_like(acc_o)

    def body(i, at):
        x = x_ref[at, :].astype(F32)
        xn = (x * rms_scale(x)).astype(BF16)
        mixed = mixed_ref[at, :]
        out_ref[at, :] = (x + dot(mixed, wo)).astype(BF16)
        acc[...] += dot_lt(xn, back_ref[at, :])
        acc_o[...] += dot_lt(mixed, up_ref[at, :])

    loop(G_STEP, body)
    write_grads(grads_ref, acc, acc_o)


VM = pl.BlockSpec(memory_space=pltpu.VMEM)
HB = pl.BlockSpec(memory_space=pltpu.HBM)
SM = pl.BlockSpec(memory_space=pltpu.SMEM)
DMA = pltpu.SemaphoreType.DMA


def shape(dims, dtype=BF16):
    return jax.ShapeDtypeStruct(dims, dtype)


def vm(dims, dtype=BF16):
    return pltpu.VMEM(dims, dtype)


ROW = (ROWS, D)
GRADS = (2, 16, 4, 8, D)
SCORES = (ROWS // BLK, BLK, HEADS * BLK)


def call(kernel, name, mib, outs, ins, out_specs, args, scratch=(), flops=0):
    args = [
        pltpu.with_memory_space_constraint(a, pltpu.HBM) if spec is HB else a
        for a, spec in zip(args, ins)
    ]
    return pl.pallas_call(
        kernel,
        out_shape=[
            pltpu.HBM(o.shape, o.dtype) if spec is HB else o for o, spec in zip(outs, out_specs)
        ],
        in_specs=ins,
        out_specs=out_specs,
        scratch_shapes=scratch,
        compiler_params=pltpu.CompilerParams(vmem_limit_bytes=mib << 20),
        cost_estimate=pl.CostEstimate(
            flops=flops, bytes_accessed=8 << 20, transcendentals=1 << 20
        ),
        name=name,
    )(*args)


def time_forward(x, w):
    return call(
        time_forward_kernel, "time_forward", 24, [shape((L, CH, D))], [HB, HB], [HB], (x, w),
        [vm(ROW), vm((4, D, D)), vm((L, CH, D)), DMA, DMA((2,)), DMA((2,))],
        flops=2 * 10**9,
    )[0]


def prepare(x, w):
    names = [shape(ROW), shape((D, ROWS)), shape(SCORES)] + [shape(ROW)] * 4 + [shape((D, ROWS))]
    return call(
        prepare_kernel, "prepare", 28, names, [VM] * 2, [VM] + [HB] * 7, (x, w),
        [vm(o.shape) for o in names[1:]] + [DMA((7, ROWS // PREP_STEP))],
        flops=3 * 10**9,
    )


def channel(nb, x, up, w):
    return call(
        channel_kernel, "channel", 48,
        [shape(ROW), shape((ROWS, 3 * D)), shape(ROW)],
        [SM, VM, HB, HB], [HB] * 3, (nb, x, up, w),
        [vm(ROW), vm((4, D, D)), DMA, DMA]
        + [vm(ROW), vm((ROWS, 3 * D)), vm(ROW), vm(ROW), vm(ROW), vm(ROW)]
        + [vm((D, ROWS))] * 2 + [vm(ROW)] * 2 + [vm(ROW, F32)] * 3 + [DMA((2,)), DMA((2,)), DMA],
        flops=8 * 10**9,
    )


def channel_grads(x, up, back, mixed, w):
    return call(
        channel_grads_kernel, "channel_grads", 20, [shape(ROW), shape(GRADS)],
        [VM] * 5, [VM] * 2, (x, up, back, mixed, w),
        [vm((D, 3 * D), F32), vm((D, D), F32)], flops=2 * 10**9,
    )


def time_backward(sg, kept, w):
    return call(
        time_backward_kernel, "time_backward", 30, [shape((ROWS, 3 * D)), shape(GRADS)],
        [VM, HB, VM] + [HB] * 7, [HB, VM], (sg, w[3]) + tuple(kept),
        [vm((D, D))] + [vm(k.shape) for k in kept[1:]]
        + [vm((ROWS, 3 * D)), vm((D, 3 * D), F32), vm((D, D), F32)]
        + [DMA, DMA((7, ROWS // T_STEP)), DMA((ROWS // T_STEP,))],
        flops=4 * 10**9,
    )


def series_gradient(x, sg, back, w):
    return call(
        series_grad_kernel, "series_grad", 20, [shape(ROW)], [VM] * 4, [VM], (x, sg, back, w),
        flops=10**9,
    )[0]


def exchange(x, axis, groups=None):
    return lax.all_to_all(
        x, axis, split_axis=0, concat_axis=0, tiled=True, axis_index_groups=groups
    )


def other_core(x):
    return lax.ppermute(x, "dp", [(i, i ^ 1) for i in range(16)])


def add_cores(parts, core):
    mine = lax.dynamic_index_in_dim(parts, core, 0, keepdims=False)
    theirs = lax.dynamic_index_in_dim(other_core(parts), core, 0, keepdims=False)
    return (mine.astype(F32) + theirs.astype(F32)).astype(BF16)


CHIPS = [[i for i in range(16) if i % 2 == c] for c in range(2)]


def reduce_grads(halves, core, beside):
    rows = exchange(halves, "mp")
    halves_first = lambda a: lax.optimization_barrier((a, halves))[0]
    other = beside(halves_first)
    rows, other = lax.optimization_barrier((rows, other))
    mine = jnp.sum(rows.astype(F32), axis=0).astype(BF16)
    every = exchange(jnp.broadcast_to(mine[None], (8,) + mine.shape), "dp", CHIPS)
    total = jnp.sum(every.astype(F32), axis=0).astype(BF16)
    theirs = other_core(total)
    low = jnp.where(core == 0, total, theirs)
    high = jnp.where(core == 0, theirs, total)
    return jnp.concatenate([low, high], axis=1).astype(F32) * (1.0 / 16), other


def shards(series, upstream_grad, time_weights, channel_weights, neighbors):
    core = lax.axis_index("dp") & 1
    x = series.reshape(ROWS, D)
    up = upstream_grad.reshape(ROWS, D)
    stream = exchange(time_forward(x, time_weights), "mp").reshape(ROWS, D)
    sg, back, mixed = channel(neighbors, stream, up, channel_weights)
    x, sg = lax.optimization_barrier((x, sg))
    returned = exchange(sg.reshape(16, CH, D), "mp")
    out, channel_parts = channel_grads(stream, up, back, mixed, channel_weights)
    channel_half = add_cores(channel_parts, core)
    kept = prepare(x, time_weights)
    returned, channel_half, kept = lax.optimization_barrier((returned, channel_half, kept))
    time_back, time_parts = time_backward(returned, kept, time_weights)
    halves = jnp.concatenate([channel_half, add_cores(time_parts, core)], axis=1)
    sums, series_grad = reduce_grads(
        halves, core, lambda gate: series_gradient(x, returned, gate(time_back), time_weights)
    )
    return (
        out.reshape(1, ROWS, 1, D),
        series_grad.reshape(1, CH, L, D),
        sums[4:],
        sums[:4],
    )


def solution(mesh):
    placed = (P("dp", "mp", None, None), P("dp", None, "mp", None), P(), P(), P())
    return jax.shard_map(
        shards,
        mesh=mesh,
        in_specs=placed,
        out_specs=(
            P("dp", None, "mp", None),
            P("dp", "mp", None, None),
            P(None, "mp", None),
            P(None, "mp", None),
        ),
        check_vma=False,
    )
```

```python
import jax
import jax.numpy as jnp
from jax import lax
from jax.experimental import pallas as pl
from jax.experimental.pallas import tpu as pltpu
from jax.sharding import PartitionSpec as P

HEADS = 4
D = 256
HD = D // HEADS
L = 16
CH = 128
BLK = 128
NBR = 3
ROWS = 2048
SQ = 256
GROUPS = 4
EPS = 1e-06
LOG2E = 1.4426950408889634
LN2 = 0.6931471805599453
QSCALE = 0.25 * LOG2E
F32 = jnp.float32
BF16 = jnp.bfloat16


def dot(a, b):
    return lax.dot_general(a, b, (((1,), (0,)), ((), ())), preferred_element_type=F32)


def dot_rt(a, b):
    return lax.dot_general(a, b, (((1,), (1,)), ((), ())), preferred_element_type=F32)


def dot_lt(a, b):
    return lax.dot_general(a, b, (((0,), (0,)), ((), ())), preferred_element_type=F32)


def iota(shape, dim):
    return lax.broadcasted_iota(jnp.int32, shape, dim)


def div(a, n):
    return lax.shift_right_logical(a, jnp.int32(n.bit_length() - 1))


def head_mean_matrix():
    same = div(iota((D, D), 0), HD) == div(iota((D, D), 1), HD)
    return jnp.where(same, 1.0 / HD, 0.0).astype(BF16)


def swap_matrix():
    row, col = iota((D, D), 0), iota((D, D), 1)
    same = (div(row, L) == (col & (L - 1))) & ((row & (L - 1)) == div(col, L))
    return jnp.where(same, 1.0, 0.0).astype(BF16)


def rms_scale(x):
    return lax.rsqrt(jnp.mean(x * x, axis=-1, keepdims=True) + EPS)


def head_scale(raw, means):
    return lax.rsqrt(dot((raw * raw).astype(BF16), means) + EPS)


def project(xn, wqkv, means):
    qkv = dot(xn, wqkv)
    raw_q, raw_k = qkv[:, :D], qkv[:, D : 2 * D]
    rq, rk = head_scale(raw_q, means), head_scale(raw_k, means)
    qs = (raw_q * (rq * QSCALE)).astype(BF16)
    kn = (raw_k * rk).astype(BF16)
    return qs, kn, qkv[:, 2 * D :].astype(BF16), rq, rk


def head_masks(rows):
    lane = div(iota((rows, D), 1), HD)
    return [lane == h for h in range(HEADS)]


def stack_heads(x, masks):
    zero = jnp.zeros_like(x)
    return jnp.concatenate([jnp.where(m, x, zero) for m in masks], axis=0)


def time_diag():
    row, col = iota((BLK, HEADS * BLK), 0), iota((BLK, HEADS * BLK), 1)
    return jnp.where(div(row, L) == div(col & (BLK - 1), L), 1.0, 0.0).astype(F32)


def head_columns():
    return [slice(h * BLK, (h + 1) * BLK) for h in range(HEADS)]


def stack_product(xts, parts):
    out = []
    for xt, p in zip(xts, parts):
        heads = [dot(xt[h * HD : (h + 1) * HD], p[:, c]) for h, c in enumerate(head_columns())]
        out.append(jnp.concatenate(heads, axis=0).T)
    return out


def softmax_columns(es):
    return [e * (1.0 / jnp.sum(e, axis=0, keepdims=True)) for e in es]


def score_grads(ps, dps):
    ts = [p * dp for p, dp in zip(ps, dps)]
    return [
        (t - p * jnp.sum(t, axis=0, keepdims=True)).astype(BF16) for t, p in zip(ts, ps)
    ]


def split(x, size=BLK):
    return [x[i : i + size] for i in range(0, x.shape[0], size)]


def join(parts):
    return jnp.concatenate(parts, axis=0)


def load_wqkv(w_ref):
    return jnp.concatenate([w_ref[0], w_ref[1], w_ref[2]], axis=1)


def loop(size, body):
    def step(i, carry):
        body(i, pl.ds(pl.multiple_of(i * size, size), size))
        return carry

    lax.fori_loop(0, ROWS // size, step, 0)


def copies(src, dst, sems, size):
    return [
        pltpu.make_async_copy(
            src.at[pl.ds(i * size, size)], dst.at[pl.ds(i * size, size)], sems.at[i]
        )
        for i in range(ROWS // size)
    ]


def kept_copies(srcs, dsts, sems, size):
    out = []
    for i in range(ROWS // size):
        step = []
        for n, (src, dst) in enumerate(zip(srcs, dsts)):
            rows = size // BLK if len(src.shape) == 3 else size
            at = (slice(None), pl.ds(i * rows, rows)) if src.shape[0] == D else pl.ds(i * rows, rows)
            step.append(pltpu.make_async_copy(src.at[at], dst.at[at], sems.at[n, i]))
        out.append(step)
    return out


A_PARTS = (1024, 1024)


def time_forward_kernel(x_hbm, w_hbm, out_hbm, x_ref, w_ref, out_ref, w_sem, in_sem, out_sem):
    w_in = pltpu.make_async_copy(w_hbm, w_ref, w_sem)
    spans, at = [], 0
    for size in A_PARTS:
        spans.append((at, size))
        at += size
    x_in = [
        pltpu.make_async_copy(x_hbm.at[pl.ds(at, n)], x_ref.at[pl.ds(at, n)], in_sem.at[i])
        for i, (at, n) in enumerate(spans)
    ]
    x_in[0].start()
    w_in.start()
    for c in x_in[1:]:
        c.start()
    means, swap = head_mean_matrix(), swap_matrix()
    masks = head_masks(BLK)
    diag = time_diag()
    outs = []
    for i, (start, size) in enumerate(spans):
        x_in[i].wait()
        if i == 0:
            w_in.wait()
            wqkv = load_wqkv(w_ref)
            wo = w_ref[3]
        x = x_ref[start : start + size, :].astype(F32)
        xn = (x * rms_scale(x)).astype(BF16)
        qs, kn, v, _, _ = project(xn, wqkv, means)
        es = [
            jnp.exp2(dot_rt(k, stack_heads(q, masks))) * diag
            for q, k in zip(split(qs), split(kn))
        ]
        pbs = [p.astype(BF16) for p in softmax_columns(es)]
        mixed = join(stack_product([u.T for u in split(v)], pbs)).astype(BF16)
        stream = (x + dot(mixed, wo)).astype(BF16)
        for j, part in enumerate(split(stream, SQ)):
            at = start // L + j * L
            out_ref[:, at : at + L, :] = dot(swap, part).astype(BF16).reshape(L, L, D)
        at = pl.ds(start // L, size // L)
        c = pltpu.make_async_copy(out_ref.at[:, at], out_hbm.at[:, at], out_sem.at[i])
        c.start()
        outs.append(c)
    for c in outs:
        c.wait()


PREP_STEP = 512


def prepare_kernel(x_ref, w_ref, *refs):
    outs, (v_ref, r_ref, xt_ref, p_ref, qs_ref, kn_ref, mt_ref), sems = (
        refs[:7], refs[7:14], refs[14],
    )
    row, col = iota((D, BLK), 0), iota((D, BLK), 1)
    pick_q = jnp.where(row == col * HD, 1.0, 0.0).astype(BF16)
    pick_k = jnp.where(row == (col - HEADS) * HD, 1.0, 0.0).astype(BF16)
    means = head_mean_matrix()
    masks = head_masks(BLK)
    diag = time_diag()
    wqkv = load_wqkv(w_ref)
    groups = PREP_STEP // BLK
    moves = kept_copies(refs[7:14], outs, sems, PREP_STEP)
    for i in range(ROWS // PREP_STEP):
        at = slice(i * PREP_STEP, (i + 1) * PREP_STEP)
        x = x_ref[at, :].astype(F32)
        xn = (x * rms_scale(x)).astype(BF16)
        qs, kn, v, rq, rk = project(xn, wqkv, means)
        xt_ref[:, at] = xn.T
        qs_ref[at, :] = qs
        kn_ref[at, :] = kn
        v_ref[at, :] = v
        r_ref[at, :] = (dot(rq.astype(BF16), pick_q) + dot(rk.astype(BF16), pick_k)).astype(BF16)
        es = [
            jnp.exp2(dot_rt(k, stack_heads(q, masks))) * diag
            for q, k in zip(split(qs), split(kn))
        ]
        pbs = [p.astype(BF16) for p in softmax_columns(es)]
        p_ref[i * groups : (i + 1) * groups] = jnp.stack(pbs)
        os = stack_product([u.T for u in split(v)], pbs)
        mt_ref[:, at] = join(os).astype(BF16).T
        for c in moves[i]:
            c.start()
    for step in moves:
        for c in step:
            c.wait()


def head_back(r, y, g, means, scale):
    yf = y.astype(F32)
    m = dot((yf * g).astype(BF16), means)
    return r * (g - yf * (m * scale))


def query_back(rq, qs, dq, means):
    return head_back(rq, qs, dq, means, 1.0 / (QSCALE * QSCALE)).astype(BF16)


def key_back(rk, kn, dk, means):
    return head_back(rk * LN2, kn, dk, means, 1.0).astype(BF16)


def rms_back(x, r, ng):
    xh = x * r
    return r * (ng - xh * jnp.mean(xh * ng, axis=-1, keepdims=True))


def write_grads(core_ref, mine_ref, theirs_ref, acc, acc_o):
    first = core_ref[0] == 0
    for j in range(4):
        whole = (acc[:, j * D : (j + 1) * D] if j < 3 else acc_o[...]).reshape(16, 2, 8, D)
        low, high = whole[:, 0], whole[:, 1]
        mine_ref[:, j] = jnp.where(first, low, high).astype(BF16)
        theirs_ref[:, j] = jnp.where(first, high, low).astype(BF16)


T_STEP = 1024


def time_backward_kernel(core_ref, sg_ref, w_hbm, *refs):
    kept_hbm, back_hbm, mine_ref, theirs_ref = refs[:7], refs[7], refs[8], refs[9]
    w_ref, kept, back_ref, acc, acc_o = refs[10], refs[11:18], refs[18], refs[19], refs[20]
    w_sem, in_sem, out_sem = refs[21:]
    v_ref, r_ref, xt_ref, p_ref, qs_ref, kn_ref, mt_ref = kept
    spread = jnp.where(
        iota((BLK, 2 * D), 0) == div(iota((BLK, 2 * D), 1), HD), 1.0, 0.0
    ).astype(BF16)
    w_in = pltpu.make_async_copy(w_hbm, w_ref, w_sem)
    w_in.start()
    moves = kept_copies(kept_hbm, kept, in_sem, T_STEP)
    for c in moves[0]:
        c.start()
    back_out = copies(back_ref, back_hbm, out_sem, T_STEP)
    means, swap = head_mean_matrix(), swap_matrix()
    masks = head_masks(BLK)
    groups, chans = T_STEP // BLK, T_STEP // L
    w_in.wait()
    wo = w_ref[...]
    for i in range(ROWS // T_STEP):
        at = slice(i * T_STEP, (i + 1) * T_STEP)
        sg = []
        for j in range(T_STEP // SQ):
            part = sg_ref[:, i * chans + j * L : i * chans + (j + 1) * L, :]
            sg.append(dot(swap, part.reshape(SQ, D)).astype(BF16))
        sg = join(sg)
        do = dot_rt(sg, wo).astype(BF16)
        for c in moves[i]:
            c.wait()
        for c in moves[i + 1] if i + 1 < len(moves) else []:
            c.start()
        qs, kn = qs_ref[at, :], kn_ref[at, :]
        pbs = [p_ref[i * groups + g] for g in range(groups)]
        dosts = [stack_heads(d, masks) for d in split(do)]
        dps = [dot_rt(v, d) for v, d in zip(split(v_ref[at, :]), dosts)]
        dss = score_grads([p.astype(F32) for p in pbs], dps)
        vb = join([dot(p, d).astype(BF16) for p, d in zip(pbs, dosts)])
        dk = join([dot(ds, stack_heads(q, masks)) for ds, q in zip(dss, split(qs))])
        dq = join(stack_product([k.T for k in split(kn)], dss))
        r = dot(r_ref[at, :], spread)
        qb = query_back(r[:, :D] * 0.25, qs, dq, means)
        kb = key_back(r[:, D:], kn, dk, means)
        back = jnp.concatenate([qb, kb, vb], axis=1)
        back_ref[at, :] = back
        back_out[i].start()
        part, part_o = dot(xt_ref[:, at], back), dot(mt_ref[:, at], sg)
        acc[...] = part if i == 0 else acc[...] + part
        acc_o[...] = part_o if i == 0 else acc_o[...] + part_o
    write_grads(core_ref, mine_ref, theirs_ref, acc, acc_o)
    for c in back_out:
        c.wait()


S_STEP = 512


def series_grad_kernel(x_ref, sg_ref, back_ref, w_ref, out_ref):
    swap = swap_matrix()
    wqkv = load_wqkv(w_ref)
    chans = S_STEP // L

    def body(i, at):
        x = x_ref[at, :].astype(F32)
        sg = []
        for j in range(S_STEP // SQ):
            part = sg_ref[:, pl.ds(pl.multiple_of(i * chans + j * L, L), L), :]
            sg.append(dot(swap, part.reshape(SQ, D)))
        ng = dot_rt(back_ref[at, :], wqkv)
        out_ref[at, :] = (join(sg) + rms_back(x, rms_scale(x), ng)).astype(BF16)

    loop(S_STEP, body)


C_STEP = 1024


def channel_kernel(
    nb_ref, x_ref, up_hbm, do_hbm, w_hbm, sg_hbm, back_hbm, mixed_hbm,
    up_ref, do_ref, w_ref, up_sem, do_sem, w_sem, sg_s, back_s, mixed_s, qs_s, kn_s, v_s, kt_s, vt_s, rq_s, rk_s, dq_s, dk_s, dv_s,
    sg_sem, back_sem, mixed_sem,
):
    w_in = pltpu.make_async_copy(w_hbm.at[pl.ds(0, 3)], w_ref, w_sem)
    w_in.start()
    up_in = pltpu.make_async_copy(up_hbm, up_ref, up_sem)
    do_in = pltpu.make_async_copy(do_hbm, do_ref, do_sem)
    do_in.start()
    up_in.start()
    means = head_mean_matrix()
    masks = head_masks(BLK)
    w_in.wait()
    wqkv = load_wqkv(w_ref)

    def first(i, at):
        x = x_ref[at, :].astype(F32)
        xn = (x * rms_scale(x)).astype(BF16)
        qs, kn, v, rq, rk = project(xn, wqkv, means)
        rq_s[at, :] = rq.astype(BF16)
        rk_s[at, :] = rk.astype(BF16)
        qs_s[at, :] = qs
        kn_s[at, :] = kn
        v_s[at, :] = v
        kt_s[:, at] = kn.T
        vt_s[:, at] = v.T
        dk_s[at, :] = jnp.zeros((C_STEP, D), F32)
        dv_s[at, :] = jnp.zeros((C_STEP, D), F32)

    loop(C_STEP, first)
    do_in.wait()
    up_in.wait()

    def attend(i, carry):
        bs = [i * GROUPS + g for g in range(GROUPS)]
        ats = [pl.ds(pl.multiple_of(b * BLK, BLK), BLK) for b in bs]
        nears = [
            [pl.ds(pl.multiple_of(nb_ref[b, j] * BLK, BLK), BLK) for j in range(NBR)] for b in bs
        ]
        qsts = [stack_heads(qs_s[at, :], masks) for at in ats]
        es = [
            jnp.exp2(dot_rt(join([kn_s[n, :] for n in near]), q))
            for near, q in zip(nears, qsts)
        ]
        dosts = [stack_heads(do_ref[at, :], masks) for at in ats]
        dps = [dot_rt(join([v_s[n, :] for n in near]), d) for near, d in zip(nears, dosts)]
        ps = softmax_columns(es)
        pbs = [p.astype(BF16) for p in ps]
        dss = score_grads(ps, dps)
        dvs = [dot(p, d) for p, d in zip(pbs, dosts)]
        os = stack_product(
            [jnp.concatenate([vt_s[:, n] for n in near], axis=1) for near in nears], pbs
        )
        dks = [dot(ds, q) for ds, q in zip(dss, qsts)]
        dqs = stack_product(
            [jnp.concatenate([kt_s[:, n] for n in near], axis=1) for near in nears], dss
        )
        for at, o, dq in zip(ats, os, dqs):
            mixed_s[at, :] = o.astype(BF16)
            dq_s[at, :] = dq
        for near, dk, dv in zip(nears, dks, dvs):
            for n, k_part, v_part in zip(near, split(dk), split(dv)):
                dk_s[n, :] += k_part
                dv_s[n, :] += v_part
        return carry

    lax.fori_loop(0, ROWS // BLK // GROUPS, attend, 0)

    mixed_out = pltpu.make_async_copy(mixed_s, mixed_hbm, mixed_sem)
    mixed_out.start()
    sg_out = copies(sg_s, sg_hbm, sg_sem, C_STEP)
    back_out = copies(back_s, back_hbm, back_sem, C_STEP)
    for i in range(ROWS // C_STEP):
        at = slice(i * C_STEP, (i + 1) * C_STEP)
        x = x_ref[at, :].astype(F32)
        r = rms_scale(x)
        qb = query_back(rq_s[at, :].astype(F32) * 0.25, qs_s[at, :], dq_s[at, :], means)
        kb = key_back(rk_s[at, :].astype(F32), kn_s[at, :], dk_s[at, :], means)
        back = jnp.concatenate([qb, kb, dv_s[at, :].astype(BF16)], axis=1)
        back_s[at, :] = back
        back_out[i].start()
        dx = rms_back(x, r, dot_rt(back, wqkv))
        sg_s[at, :] = (up_ref[at, :].astype(F32) + dx).astype(BF16)
        sg_out[i].start()
    mixed_out.wait()
    for c in back_out + sg_out:
        c.wait()


G_STEP = 512


def channel_grads_kernel(
    core_ref, x_ref, up_ref, back_ref, mixed_ref, w_ref, out_ref, mine_ref, theirs_ref, acc, acc_o
):
    wo = w_ref[3]
    acc[...] = jnp.zeros_like(acc)
    acc_o[...] = jnp.zeros_like(acc_o)

    def body(i, at):
        x = x_ref[at, :].astype(F32)
        xn = (x * rms_scale(x)).astype(BF16)
        mixed = mixed_ref[at, :]
        out_ref[at, :] = (x + dot(mixed, wo)).astype(BF16)
        acc[...] += dot_lt(xn, back_ref[at, :])
        acc_o[...] += dot_lt(mixed, up_ref[at, :])

    loop(G_STEP, body)
    write_grads(core_ref, mine_ref, theirs_ref, acc, acc_o)


VM = pl.BlockSpec(memory_space=pltpu.VMEM)
HB = pl.BlockSpec(memory_space=pltpu.HBM)
SM = pl.BlockSpec(memory_space=pltpu.SMEM)
DMA = pltpu.SemaphoreType.DMA


def shape(dims, dtype=BF16):
    return jax.ShapeDtypeStruct(dims, dtype)


def vm(dims, dtype=BF16):
    return pltpu.VMEM(dims, dtype)


ROW = (ROWS, D)
GRADS = (16, 4, 8, D)
SCORES = (ROWS // BLK, BLK, HEADS * BLK)


def call(kernel, name, mib, outs, ins, out_specs, args, scratch=(), flops=0):
    args = [
        pltpu.with_memory_space_constraint(a, pltpu.HBM) if spec is HB else a
        for a, spec in zip(args, ins)
    ]
    return pl.pallas_call(
        kernel,
        out_shape=[
            pltpu.HBM(o.shape, o.dtype) if spec is HB else o for o, spec in zip(outs, out_specs)
        ],
        in_specs=ins,
        out_specs=out_specs,
        scratch_shapes=scratch,
        compiler_params=pltpu.CompilerParams(vmem_limit_bytes=mib << 20),
        cost_estimate=pl.CostEstimate(
            flops=flops, bytes_accessed=8 << 20, transcendentals=1 << 20
        ),
        name=name,
    )(*args)


def time_forward(x, w):
    return call(
        time_forward_kernel, "time_forward", 24, [shape((L, CH, D))], [HB, HB], [HB], (x, w),
        [vm(ROW), vm((4, D, D)), vm((L, CH, D)), DMA, DMA((len(A_PARTS),)), DMA((len(A_PARTS),))],
        flops=2 * 10**9,
    )[0]


def prepare(x, w):
    cols = shape((D, ROWS))
    names = [shape(ROW), shape((ROWS, BLK)), cols, shape(SCORES), shape(ROW), shape(ROW), cols]
    return call(
        prepare_kernel, "prepare", 28, names, [VM] * 2, [HB] * 7, (x, w),
        [vm(o.shape) for o in names] + [DMA((7, ROWS // PREP_STEP))],
        flops=3 * 10**9,
    )


def output_back_kernel(up_ref, w_ref, do_ref):
    wo = w_ref[3]

    def body(i, at):
        do_ref[at, :] = dot_rt(up_ref[at, :], wo).astype(BF16)

    loop(512, body)


def output_back(up, w):
    return call(
        output_back_kernel, "output_back", 16, [shape(ROW)], [VM] * 2, [VM], (up, w),
        flops=10**9,
    )[0]


def channel(nb, x, up, do, w):
    return call(
        channel_kernel, "channel", 48,
        [shape(ROW), shape((ROWS, 3 * D)), shape(ROW)],
        [SM, VM, HB, HB, HB], [HB] * 3, (nb, x, up, do, w),
        [vm(ROW), vm(ROW), vm((3, D, D)), DMA, DMA, DMA]
        + [vm(ROW), vm((ROWS, 3 * D)), vm(ROW), vm(ROW), vm(ROW), vm(ROW)]
        + [vm((D, ROWS))] * 2 + [vm(ROW)] * 2 + [vm(ROW, F32)] * 3 + [DMA((2,)), DMA((2,)), DMA],
        flops=8 * 10**9,
    )


def channel_grads(core, x, up, back, mixed, w):
    return call(
        channel_grads_kernel, "channel_grads", 20, [shape(ROW), shape(GRADS), shape(GRADS)],
        [SM] + [VM] * 5, [VM] * 3, (core, x, up, back, mixed, w),
        [vm((D, 3 * D), F32), vm((D, D), F32)], flops=2 * 10**9,
    )


def time_backward(core, sg, kept, w):
    return call(
        time_backward_kernel, "time_backward", 30, [shape((ROWS, 3 * D)), shape(GRADS), shape(GRADS)],
        [SM, VM, HB] + [HB] * 7, [HB, VM, VM], (core, sg, w[3]) + tuple(kept),
        [vm((D, D))] + [vm(k.shape) for k in kept]
        + [vm((ROWS, 3 * D)), vm((D, 3 * D), F32), vm((D, D), F32)]
        + [DMA, DMA((7, ROWS // T_STEP)), DMA((ROWS // T_STEP,))],
        flops=4 * 10**9,
    )


def series_gradient(x, sg, back, w):
    return call(
        series_grad_kernel, "series_grad", 20, [shape(ROW)], [VM] * 4, [VM], (x, sg, back, w),
        flops=10**9,
    )[0]


def exchange(x, axis, groups=None):
    return lax.all_to_all(
        x, axis, split_axis=0, concat_axis=0, tiled=True, axis_index_groups=groups
    )


def other_core(x):
    return lax.ppermute(x, "dp", [(i, i ^ 1) for i in range(16)])


def add_cores(mine, theirs):
    return (mine.astype(F32) + other_core(theirs).astype(F32)).astype(BF16)


CHIPS = [[i for i in range(16) if i % 2 == c] for c in range(2)]


def reduce_grads(halves, core, beside):
    rows = exchange(halves, "mp")
    halves_first = lambda a: lax.optimization_barrier((a, halves))[0]
    other = beside(halves_first)
    rows, other = lax.optimization_barrier((rows, other))
    mine = jnp.sum(rows.astype(F32), axis=0).astype(BF16)
    every = exchange(jnp.broadcast_to(mine[None], (8,) + mine.shape), "dp", CHIPS)
    total = jnp.sum(every.astype(F32), axis=0).astype(BF16)
    theirs = other_core(total)
    low = jnp.where(core == 0, total, theirs)
    high = jnp.where(core == 0, theirs, total)
    return jnp.concatenate([low, high], axis=1).astype(F32) * (1.0 / 16), other


def shards(series, upstream_grad, time_weights, channel_weights, neighbors):
    core = lax.axis_index("dp") & 1
    x = series.reshape(ROWS, D)
    up = upstream_grad.reshape(ROWS, D)
    stream = exchange(time_forward(x, time_weights), "mp").reshape(ROWS, D)
    do = output_back(up, channel_weights)
    sg, back, mixed = channel(neighbors, stream, up, do, channel_weights)
    x, sg = lax.optimization_barrier((x, sg))
    returned = exchange(sg.reshape(16, CH, D), "mp")
    place = core.reshape(1)
    out, *channel_parts = channel_grads(place, stream, up, back, mixed, channel_weights)
    channel_half = add_cores(*channel_parts)
    kept = prepare(x, time_weights)
    returned, channel_half, kept = lax.optimization_barrier((returned, channel_half, kept))
    time_back, *time_parts = time_backward(place, returned, kept, time_weights)
    halves = jnp.concatenate([channel_half, add_cores(*time_parts)], axis=1)
    sums, series_grad = reduce_grads(
        halves, core, lambda gate: series_gradient(x, returned, gate(time_back), time_weights)
    )
    return (
        out.reshape(1, ROWS, 1, D),
        series_grad.reshape(1, CH, L, D),
        sums[4:],
        sums[:4],
    )


def solution(mesh):
    placed = (P("dp", "mp", None, None), P("dp", None, "mp", None), P(), P(), P())
    return jax.shard_map(
        shards,
        mesh=mesh,
        in_specs=placed,
        out_specs=(
            P("dp", None, "mp", None),
            P("dp", "mp", None, None),
            P(None, "mp", None),
            P(None, "mp", None),
        ),
        check_vma=False,
    )
```

```python
import jax
import jax.numpy as jnp
from jax import lax
from jax.experimental import pallas as pl
from jax.experimental.pallas import tpu as pltpu
from jax.sharding import PartitionSpec as P

HEADS = 4
D = 256
HD = D // HEADS
L = 16
CH = 128
BLK = 128
NBR = 3
ROWS = 2048
SQ = 256
GROUPS = 4
EPS = 1e-06
LOG2E = 1.4426950408889634
LN2 = 0.6931471805599453
QSCALE = 0.25 * LOG2E
F32 = jnp.float32
BF16 = jnp.bfloat16


def dot(a, b):
    return lax.dot_general(a, b, (((1,), (0,)), ((), ())), preferred_element_type=F32)


def dot_rt(a, b):
    return lax.dot_general(a, b, (((1,), (1,)), ((), ())), preferred_element_type=F32)


def dot_lt(a, b):
    return lax.dot_general(a, b, (((0,), (0,)), ((), ())), preferred_element_type=F32)


def iota(shape, dim):
    return lax.broadcasted_iota(jnp.int32, shape, dim)


def div(a, n):
    return lax.shift_right_logical(a, jnp.int32(n.bit_length() - 1))


def head_mean_matrix():
    same = div(iota((D, D), 0), HD) == div(iota((D, D), 1), HD)
    return jnp.where(same, 1.0 / HD, 0.0).astype(BF16)


def swap_matrix():
    row, col = iota((D, D), 0), iota((D, D), 1)
    same = (div(row, L) == (col & (L - 1))) & ((row & (L - 1)) == div(col, L))
    return jnp.where(same, 1.0, 0.0).astype(BF16)


def rms_scale(x):
    return lax.rsqrt(jnp.mean(x * x, axis=-1, keepdims=True) + EPS)


def head_scale(raw, means):
    return lax.rsqrt(dot((raw * raw).astype(BF16), means) + EPS)


def project(xn, wqkv, means):
    qkv = dot(xn, wqkv)
    raw_q, raw_k = qkv[:, :D], qkv[:, D : 2 * D]
    rq, rk = head_scale(raw_q, means), head_scale(raw_k, means)
    qs = (raw_q * (rq * QSCALE)).astype(BF16)
    kn = (raw_k * rk).astype(BF16)
    return qs, kn, qkv[:, 2 * D :].astype(BF16), rq, rk


def head_masks(rows):
    lane = div(iota((rows, D), 1), HD)
    return [lane == h for h in range(HEADS)]


def stack_heads(x, masks):
    zero = jnp.zeros_like(x)
    return jnp.concatenate([jnp.where(m, x, zero) for m in masks], axis=0)


def time_diag():
    row, col = iota((BLK, HEADS * BLK), 0), iota((BLK, HEADS * BLK), 1)
    return jnp.where(div(row, L) == div(col & (BLK - 1), L), 1.0, 0.0).astype(F32)


def head_columns():
    return [slice(h * BLK, (h + 1) * BLK) for h in range(HEADS)]


def stack_product(xts, parts):
    out = []
    for xt, p in zip(xts, parts):
        heads = [dot(xt[h * HD : (h + 1) * HD], p[:, c]) for h, c in enumerate(head_columns())]
        out.append(jnp.concatenate(heads, axis=0).T)
    return out


def softmax_columns(es):
    return [e * (1.0 / jnp.sum(e, axis=0, keepdims=True)) for e in es]


def score_grads(ps, dps):
    ts = [p * dp for p, dp in zip(ps, dps)]
    return [
        (t - p * jnp.sum(t, axis=0, keepdims=True)).astype(BF16) for t, p in zip(ts, ps)
    ]


def split(x, size=BLK):
    return [x[i : i + size] for i in range(0, x.shape[0], size)]


def join(parts):
    return jnp.concatenate(parts, axis=0)


def load_wqkv(w_ref):
    return jnp.concatenate([w_ref[0], w_ref[1], w_ref[2]], axis=1)


def loop(size, body):
    def step(i, carry):
        body(i, pl.ds(pl.multiple_of(i * size, size), size))
        return carry

    lax.fori_loop(0, ROWS // size, step, 0)


def copies(src, dst, sems, size):
    return [
        pltpu.make_async_copy(
            src.at[pl.ds(i * size, size)], dst.at[pl.ds(i * size, size)], sems.at[i]
        )
        for i in range(ROWS // size)
    ]


def kept_copies(srcs, dsts, sems, size):
    out = []
    for i in range(ROWS // size):
        step = []
        for n, (src, dst) in enumerate(zip(srcs, dsts)):
            rows = size // BLK if len(src.shape) == 3 else size
            at = (slice(None), pl.ds(i * rows, rows)) if src.shape[0] == D else pl.ds(i * rows, rows)
            step.append(pltpu.make_async_copy(src.at[at], dst.at[at], sems.at[n, i]))
        out.append(step)
    return out


A_PARTS = (1024, 1024)


def time_forward_kernel(x_hbm, w_hbm, out_hbm, x_ref, w_ref, out_ref, w_sem, in_sem, out_sem):
    w_in = pltpu.make_async_copy(w_hbm, w_ref, w_sem)
    spans, at = [], 0
    for size in A_PARTS:
        spans.append((at, size))
        at += size
    x_in = [
        pltpu.make_async_copy(x_hbm.at[pl.ds(at, n)], x_ref.at[pl.ds(at, n)], in_sem.at[i])
        for i, (at, n) in enumerate(spans)
    ]
    x_in[0].start()
    w_in.start()
    for c in x_in[1:]:
        c.start()
    means, swap = head_mean_matrix(), swap_matrix()
    masks = head_masks(BLK)
    diag = time_diag()
    outs = []
    for i, (start, size) in enumerate(spans):
        x_in[i].wait()
        if i == 0:
            w_in.wait()
            wqkv = load_wqkv(w_ref)
            wo = w_ref[3]
        x = x_ref[start : start + size, :].astype(F32)
        xn = (x * rms_scale(x)).astype(BF16)
        qs, kn, v, _, _ = project(xn, wqkv, means)
        es = [
            jnp.exp2(dot_rt(k, stack_heads(q, masks))) * diag
            for q, k in zip(split(qs), split(kn))
        ]
        pbs = [p.astype(BF16) for p in softmax_columns(es)]
        mixed = join(stack_product([u.T for u in split(v)], pbs)).astype(BF16)
        stream = (x + dot(mixed, wo)).astype(BF16)
        for j, part in enumerate(split(stream, SQ)):
            at = start // L + j * L
            out_ref[:, at : at + L, :] = dot(swap, part).astype(BF16).reshape(L, L, D)
        at = pl.ds(start // L, size // L)
        c = pltpu.make_async_copy(out_ref.at[:, at], out_hbm.at[:, at], out_sem.at[i])
        c.start()
        outs.append(c)
    for c in outs:
        c.wait()


PREP_STEP = 512


def prepare_kernel(x_ref, w_ref, *refs):
    outs, (v_ref, r_ref, xt_ref, p_ref, qs_ref, kn_ref, mt_ref), sems = (
        refs[:7], refs[7:14], refs[14],
    )
    row, col = iota((D, BLK), 0), iota((D, BLK), 1)
    pick_q = jnp.where(row == col * HD, 1.0, 0.0).astype(BF16)
    pick_k = jnp.where(row == (col - HEADS) * HD, 1.0, 0.0).astype(BF16)
    means = head_mean_matrix()
    masks = head_masks(BLK)
    diag = time_diag()
    wqkv = load_wqkv(w_ref)
    groups = PREP_STEP // BLK
    moves = kept_copies(refs[7:14], outs, sems, PREP_STEP)
    for i in range(ROWS // PREP_STEP):
        at = slice(i * PREP_STEP, (i + 1) * PREP_STEP)
        x = x_ref[at, :].astype(F32)
        xn = (x * rms_scale(x)).astype(BF16)
        qs, kn, v, rq, rk = project(xn, wqkv, means)
        xt_ref[:, at] = xn.T
        qs_ref[at, :] = qs
        kn_ref[at, :] = kn
        v_ref[at, :] = v
        r_ref[at, :] = (dot(rq.astype(BF16), pick_q) + dot(rk.astype(BF16), pick_k)).astype(BF16)
        es = [
            jnp.exp2(dot_rt(k, stack_heads(q, masks))) * diag
            for q, k in zip(split(qs), split(kn))
        ]
        pbs = [p.astype(BF16) for p in softmax_columns(es)]
        p_ref[i * groups : (i + 1) * groups] = jnp.stack(pbs)
        os = stack_product([u.T for u in split(v)], pbs)
        mt_ref[:, at] = join(os).astype(BF16).T
        for c in moves[i]:
            c.start()
    for step in moves:
        for c in step:
            c.wait()


def head_back(r, y, g, means, scale):
    yf = y.astype(F32)
    m = dot((yf * g).astype(BF16), means)
    return r * (g - yf * (m * scale))


def query_back(rq, qs, dq, means):
    return head_back(rq, qs, dq, means, 1.0 / (QSCALE * QSCALE)).astype(BF16)


def key_back(rk, kn, dk, means):
    return head_back(rk * LN2, kn, dk, means, 1.0).astype(BF16)


def rms_back(x, r, ng):
    xh = x * r
    return r * (ng - xh * jnp.mean(xh * ng, axis=-1, keepdims=True))


def write_grads(core_ref, mine_ref, theirs_ref, acc, acc_o):
    first = core_ref[0] == 0
    for j in range(4):
        whole = (acc[:, j * D : (j + 1) * D] if j < 3 else acc_o[...]).reshape(16, 2, 8, D)
        low, high = whole[:, 0], whole[:, 1]
        mine_ref[:, j] = jnp.where(first, low, high).astype(BF16)
        theirs_ref[:, j] = jnp.where(first, high, low).astype(BF16)


T_STEP = 1024


def time_backward_kernel(core_ref, sg_ref, w_hbm, *refs):
    kept_hbm, back_hbm, mine_ref, theirs_ref = refs[:7], refs[7], refs[8], refs[9]
    w_ref, kept, back_ref, acc, acc_o = refs[10], refs[11:18], refs[18], refs[19], refs[20]
    w_sem, in_sem, out_sem = refs[21:]
    v_ref, r_ref, xt_ref, p_ref, qs_ref, kn_ref, mt_ref = kept
    spread = jnp.where(
        iota((BLK, 2 * D), 0) == div(iota((BLK, 2 * D), 1), HD), 1.0, 0.0
    ).astype(BF16)
    w_in = pltpu.make_async_copy(w_hbm, w_ref, w_sem)
    w_in.start()
    moves = kept_copies(kept_hbm, kept, in_sem, T_STEP)
    for c in moves[0]:
        c.start()
    back_out = copies(back_ref, back_hbm, out_sem, T_STEP)
    means, swap = head_mean_matrix(), swap_matrix()
    masks = head_masks(BLK)
    groups, chans = T_STEP // BLK, T_STEP // L
    w_in.wait()
    wo = w_ref[...]
    for i in range(ROWS // T_STEP):
        at = slice(i * T_STEP, (i + 1) * T_STEP)
        sg = []
        for j in range(T_STEP // SQ):
            part = sg_ref[:, i * chans + j * L : i * chans + (j + 1) * L, :]
            sg.append(dot(swap, part.reshape(SQ, D)).astype(BF16))
        sg = join(sg)
        do = dot_rt(sg, wo).astype(BF16)
        for c in moves[i]:
            c.wait()
        for c in moves[i + 1] if i + 1 < len(moves) else []:
            c.start()
        qs, kn = qs_ref[at, :], kn_ref[at, :]
        pbs = [p_ref[i * groups + g] for g in range(groups)]
        dosts = [stack_heads(d, masks) for d in split(do)]
        dps = [dot_rt(v, d) for v, d in zip(split(v_ref[at, :]), dosts)]
        dss = score_grads([p.astype(F32) for p in pbs], dps)
        vb = join([dot(p, d).astype(BF16) for p, d in zip(pbs, dosts)])
        dk = join([dot(ds, stack_heads(q, masks)) for ds, q in zip(dss, split(qs))])
        dq = join(stack_product([k.T for k in split(kn)], dss))
        r = dot(r_ref[at, :], spread)
        qb = query_back(r[:, :D] * 0.25, qs, dq, means)
        kb = key_back(r[:, D:], kn, dk, means)
        back = jnp.concatenate([qb, kb, vb], axis=1)
        back_ref[at, :] = back
        back_out[i].start()
        part, part_o = dot(xt_ref[:, at], back), dot(mt_ref[:, at], sg)
        acc[...] = part if i == 0 else acc[...] + part
        acc_o[...] = part_o if i == 0 else acc_o[...] + part_o
    write_grads(core_ref, mine_ref, theirs_ref, acc, acc_o)
    for c in back_out:
        c.wait()


S_STEP = 512


def series_grad_kernel(x_ref, sg_ref, back_ref, w_ref, out_ref):
    swap = swap_matrix()
    wqkv = load_wqkv(w_ref)
    chans = S_STEP // L

    def body(i, at):
        x = x_ref[at, :].astype(F32)
        sg = []
        for j in range(S_STEP // SQ):
            part = sg_ref[:, pl.ds(pl.multiple_of(i * chans + j * L, L), L), :]
            sg.append(dot(swap, part.reshape(SQ, D)))
        ng = dot_rt(back_ref[at, :], wqkv)
        out_ref[at, :] = (join(sg) + rms_back(x, rms_scale(x), ng)).astype(BF16)

    loop(S_STEP, body)


C_STEP = 1024


def channel_kernel(
    nb_ref, x_ref, up_hbm, do_hbm, w_hbm, sg_hbm, back_hbm, mixed_hbm,
    up_ref, do_ref, w_ref, up_sem, do_sem, w_sem, sg_s, back_s, mixed_s, qs_s, kn_s, v_s, kt_s, vt_s, rq_s, rk_s, dq_s, dk_s, dv_s,
    sg_sem, back_sem, value_sem, mixed_sem,
):
    w_in = pltpu.make_async_copy(w_hbm.at[pl.ds(0, 3)], w_ref, w_sem)
    w_in.start()
    up_in = pltpu.make_async_copy(up_hbm, up_ref, up_sem)
    do_in = pltpu.make_async_copy(do_hbm, do_ref, do_sem)
    do_in.start()
    up_in.start()
    means = head_mean_matrix()
    masks = head_masks(BLK)
    w_in.wait()
    wqkv = load_wqkv(w_ref)

    def first(i, at):
        x = x_ref[at, :].astype(F32)
        xn = (x * rms_scale(x)).astype(BF16)
        qs, kn, v, rq, rk = project(xn, wqkv, means)
        rq_s[at, :] = rq.astype(BF16)
        rk_s[at, :] = rk.astype(BF16)
        qs_s[at, :] = qs
        kn_s[at, :] = kn
        v_s[at, :] = v
        kt_s[:, at] = kn.T
        vt_s[:, at] = v.T
        dk_s[at, :] = jnp.zeros((C_STEP, D), F32)
        dv_s[at, :] = jnp.zeros((C_STEP, D), F32)

    loop(C_STEP, first)
    do_in.wait()
    up_in.wait()

    def attend(i, carry):
        bs = [i * GROUPS + g for g in range(GROUPS)]
        ats = [pl.ds(pl.multiple_of(b * BLK, BLK), BLK) for b in bs]
        nears = [
            [pl.ds(pl.multiple_of(nb_ref[b, j] * BLK, BLK), BLK) for j in range(NBR)] for b in bs
        ]
        qsts = [stack_heads(qs_s[at, :], masks) for at in ats]
        es = [
            jnp.exp2(dot_rt(join([kn_s[n, :] for n in near]), q))
            for near, q in zip(nears, qsts)
        ]
        dosts = [stack_heads(do_ref[at, :], masks) for at in ats]
        dps = [dot_rt(join([v_s[n, :] for n in near]), d) for near, d in zip(nears, dosts)]
        ps = softmax_columns(es)
        pbs = [p.astype(BF16) for p in ps]
        dss = score_grads(ps, dps)
        dvs = [dot(p, d) for p, d in zip(pbs, dosts)]
        os = stack_product(
            [jnp.concatenate([vt_s[:, n] for n in near], axis=1) for near in nears], pbs
        )
        dks = [dot(ds, q) for ds, q in zip(dss, qsts)]
        dqs = stack_product(
            [jnp.concatenate([kt_s[:, n] for n in near], axis=1) for near in nears], dss
        )
        for at, o, dq in zip(ats, os, dqs):
            mixed_s[at, :] = o.astype(BF16)
            dq_s[at, :] = dq
        for near, dk, dv in zip(nears, dks, dvs):
            for n, k_part, v_part in zip(near, split(dk), split(dv)):
                dk_s[n, :] += k_part
                dv_s[n, :] += v_part
        return carry

    lax.fori_loop(0, ROWS // BLK // GROUPS, attend, 0)

    mixed_out = pltpu.make_async_copy(mixed_s, mixed_hbm, mixed_sem)
    mixed_out.start()
    sg_out = copies(sg_s, sg_hbm, sg_sem, C_STEP)
    cols, value = pl.ds(0, 2 * D), pl.ds(2 * D, D)
    value_out = copies(back_s.at[:, value], back_hbm.at[:, value], value_sem, C_STEP)
    back_out = copies(back_s.at[:, cols], back_hbm.at[:, cols], back_sem, C_STEP)
    for i in range(ROWS // C_STEP):
        at = slice(i * C_STEP, (i + 1) * C_STEP)
        back_s[at, 2 * D :] = dv_s[at, :].astype(BF16)
        value_out[i].start()
    for i in range(ROWS // C_STEP):
        at = slice(i * C_STEP, (i + 1) * C_STEP)
        x = x_ref[at, :].astype(F32)
        r = rms_scale(x)
        qb = query_back(rq_s[at, :].astype(F32) * 0.25, qs_s[at, :], dq_s[at, :], means)
        kb = key_back(rk_s[at, :].astype(F32), kn_s[at, :], dk_s[at, :], means)
        pair = jnp.concatenate([qb, kb], axis=1)
        back_s[at, : 2 * D] = pair
        back = jnp.concatenate([pair, back_s[at, 2 * D :]], axis=1)
        back_out[i].start()
        dx = rms_back(x, r, dot_rt(back, wqkv))
        sg_s[at, :] = (up_ref[at, :].astype(F32) + dx).astype(BF16)
        sg_out[i].start()
    mixed_out.wait()
    for c in value_out + back_out + sg_out:
        c.wait()


G_STEP = 512


def channel_grads_kernel(
    core_ref, x_ref, up_ref, back_ref, mixed_ref, w_ref, out_ref, mine_ref, theirs_ref, acc, acc_o
):
    wo = w_ref[3]
    acc[...] = jnp.zeros_like(acc)
    acc_o[...] = jnp.zeros_like(acc_o)

    def body(i, at):
        x = x_ref[at, :].astype(F32)
        xn = (x * rms_scale(x)).astype(BF16)
        mixed = mixed_ref[at, :]
        out_ref[at, :] = (x + dot(mixed, wo)).astype(BF16)
        acc[...] += dot_lt(xn, back_ref[at, :])
        acc_o[...] += dot_lt(mixed, up_ref[at, :])

    loop(G_STEP, body)
    write_grads(core_ref, mine_ref, theirs_ref, acc, acc_o)


VM = pl.BlockSpec(memory_space=pltpu.VMEM)
HB = pl.BlockSpec(memory_space=pltpu.HBM)
SM = pl.BlockSpec(memory_space=pltpu.SMEM)
DMA = pltpu.SemaphoreType.DMA


def shape(dims, dtype=BF16):
    return jax.ShapeDtypeStruct(dims, dtype)


def vm(dims, dtype=BF16):
    return pltpu.VMEM(dims, dtype)


ROW = (ROWS, D)
GRADS = (16, 4, 8, D)
SCORES = (ROWS // BLK, BLK, HEADS * BLK)


def call(kernel, name, mib, outs, ins, out_specs, args, scratch=(), flops=0):
    args = [
        pltpu.with_memory_space_constraint(a, pltpu.HBM) if spec is HB else a
        for a, spec in zip(args, ins)
    ]
    return pl.pallas_call(
        kernel,
        out_shape=[
            pltpu.HBM(o.shape, o.dtype) if spec is HB else o for o, spec in zip(outs, out_specs)
        ],
        in_specs=ins,
        out_specs=out_specs,
        scratch_shapes=scratch,
        compiler_params=pltpu.CompilerParams(vmem_limit_bytes=mib << 20),
        cost_estimate=pl.CostEstimate(
            flops=flops, bytes_accessed=8 << 20, transcendentals=1 << 20
        ),
        name=name,
    )(*args)


def time_forward(x, w):
    return call(
        time_forward_kernel, "time_forward", 24, [shape((L, CH, D))], [HB, HB], [HB], (x, w),
        [vm(ROW), vm((4, D, D)), vm((L, CH, D)), DMA, DMA((len(A_PARTS),)), DMA((len(A_PARTS),))],
        flops=2 * 10**9,
    )[0]


def prepare(x, w):
    cols = shape((D, ROWS))
    names = [shape(ROW), shape((ROWS, BLK)), cols, shape(SCORES), shape(ROW), shape(ROW), cols]
    return call(
        prepare_kernel, "prepare", 28, names, [VM] * 2, [HB] * 7, (x, w),
        [vm(o.shape) for o in names] + [DMA((7, ROWS // PREP_STEP))],
        flops=3 * 10**9,
    )


def output_back_kernel(up_ref, w_ref, do_ref):
    wo = w_ref[3]

    def body(i, at):
        do_ref[at, :] = dot_rt(up_ref[at, :], wo).astype(BF16)

    loop(512, body)


def output_back(up, w):
    return call(
        output_back_kernel, "output_back", 16, [shape(ROW)], [VM] * 2, [VM], (up, w),
        flops=10**9,
    )[0]


def channel(nb, x, up, do, w):
    return call(
        channel_kernel, "channel", 48,
        [shape(ROW), shape((ROWS, 3 * D)), shape(ROW)],
        [SM, VM, HB, HB, HB], [HB] * 3, (nb, x, up, do, w),
        [vm(ROW), vm(ROW), vm((3, D, D)), DMA, DMA, DMA]
        + [vm(ROW), vm((ROWS, 3 * D)), vm(ROW), vm(ROW), vm(ROW), vm(ROW)]
        + [vm((D, ROWS))] * 2 + [vm(ROW)] * 2 + [vm(ROW, F32)] * 3 + [DMA((2,)), DMA((2,)), DMA((2,)), DMA],
        flops=8 * 10**9,
    )


def channel_grads(core, x, up, back, mixed, w):
    return call(
        channel_grads_kernel, "channel_grads", 20, [shape(ROW), shape(GRADS), shape(GRADS)],
        [SM] + [VM] * 5, [VM] * 3, (core, x, up, back, mixed, w),
        [vm((D, 3 * D), F32), vm((D, D), F32)], flops=2 * 10**9,
    )


def time_backward(core, sg, kept, w):
    return call(
        time_backward_kernel, "time_backward", 30, [shape((ROWS, 3 * D)), shape(GRADS), shape(GRADS)],
        [SM, VM, HB] + [HB] * 7, [HB, VM, VM], (core, sg, w[3]) + tuple(kept),
        [vm((D, D))] + [vm(k.shape) for k in kept]
        + [vm((ROWS, 3 * D)), vm((D, 3 * D), F32), vm((D, D), F32)]
        + [DMA, DMA((7, ROWS // T_STEP)), DMA((ROWS // T_STEP,))],
        flops=4 * 10**9,
    )


def series_gradient(x, sg, back, w):
    return call(
        series_grad_kernel, "series_grad", 20, [shape(ROW)], [VM] * 4, [VM], (x, sg, back, w),
        flops=10**9,
    )[0]


def exchange(x, axis, groups=None):
    return lax.all_to_all(
        x, axis, split_axis=0, concat_axis=0, tiled=True, axis_index_groups=groups
    )


def other_core(x):
    return lax.ppermute(x, "dp", [(i, i ^ 1) for i in range(16)])


def add_cores(mine, theirs):
    return (mine.astype(F32) + other_core(theirs).astype(F32)).astype(BF16)


CHIPS = [[i for i in range(16) if i % 2 == c] for c in range(2)]


def reduce_grads(halves, core, beside):
    rows = exchange(halves, "mp")
    halves_first = lambda a: lax.optimization_barrier((a, halves))[0]
    other = beside(halves_first)
    rows, other = lax.optimization_barrier((rows, other))
    mine = jnp.sum(rows.astype(F32), axis=0).astype(BF16)
    every = exchange(jnp.broadcast_to(mine[None], (8,) + mine.shape), "dp", CHIPS)
    total = jnp.sum(every.astype(F32), axis=0).astype(BF16)
    theirs = other_core(total)
    low = jnp.where(core == 0, total, theirs)
    high = jnp.where(core == 0, theirs, total)
    return jnp.concatenate([low, high], axis=1).astype(F32) * (1.0 / 16), other


def shards(series, upstream_grad, time_weights, channel_weights, neighbors):
    core = lax.axis_index("dp") & 1
    x = series.reshape(ROWS, D)
    up = upstream_grad.reshape(ROWS, D)
    stream = exchange(time_forward(x, time_weights), "mp").reshape(ROWS, D)
    do = output_back(up, channel_weights)
    sg, back, mixed = channel(neighbors, stream, up, do, channel_weights)
    x, sg = lax.optimization_barrier((x, sg))
    returned = exchange(sg.reshape(16, CH, D), "mp")
    place = core.reshape(1)
    out, *channel_parts = channel_grads(place, stream, up, back, mixed, channel_weights)
    channel_half = add_cores(*channel_parts)
    kept = prepare(x, time_weights)
    returned, channel_half, kept = lax.optimization_barrier((returned, channel_half, kept))
    time_back, *time_parts = time_backward(place, returned, kept, time_weights)
    halves = jnp.concatenate([channel_half, add_cores(*time_parts)], axis=1)
    sums, series_grad = reduce_grads(
        halves, core, lambda gate: series_gradient(x, returned, gate(time_back), time_weights)
    )
    return (
        out.reshape(1, ROWS, 1, D),
        series_grad.reshape(1, CH, L, D),
        sums[4:],
        sums[:4],
    )


def solution(mesh):
    placed = (P("dp", "mp", None, None), P("dp", None, "mp", None), P(), P(), P())
    return jax.shard_map(
        shards,
        mesh=mesh,
        in_specs=placed,
        out_specs=(
            P("dp", None, "mp", None),
            P("dp", "mp", None, None),
            P(None, "mp", None),
            P(None, "mp", None),
        ),
        check_vma=False,
    )
```
